32 devices in a mesh: energy: 2 (over y), slab: 4 (over z), col: 2 (over x), orb: 2 (over core).
Axes of the slice: x: 2, y: 2, z: 4, core: 2. Of those that a mesh axis runs over, the one named last changes fastest.
Arguments:
- rhs: bfloat16 [2, 8, 512, 1024], P(None, ('energy', 'slab'), None, ('col', 'orb')), parts along dimension 1, may hold values from -6 to 6
- dinv: bfloat16 [2, 8, 512, 512], P(None, ('energy', 'slab'), 'orb'), parts along dimension 1, may hold values from -0.078125 to 1.125
- spikes: bfloat16 [2, 8, 2, 512, 512], P(None, ('energy', 'slab'), None, 'orb'), parts along dimension 1, may hold values from -0.09375 to 0.09375
- merge_inv: bfloat16 [2, 8, 512, 512], P(None, ('energy', 'slab'), 'orb'), parts along dimension 1, may hold values from -0.078125 to 1.125
Outputs:
- solution: float32 [2, 8, 512, 1024], P(None, ('energy', 'slab'), None, ('col', 'orb')), parts along dimension 1
The draws below stay inside these ranges and needn't reach their ends.
There are 2 independent parts, one for each index of `energy`. The reference program is written for one: setup_inputs(seed, part) draws one part's arguments, and reference() takes and returns one part's arrays. A program takes and returns all parts, laid end to end along the dimension named above; each array names one. Nothing has to cross between parts.
All inputs are finite; a program needn't handle non-finite values.
Results may differ from the reference program's by a relative error of at most 0.013.
Values may be sent and summed in bfloat16 or wider, within the bound.
No kernel may reach another device: no remote copies, remote signals or barrier semaphores. Data moves between devices by JAX's collectives and lax.ppermute only.
A program may use at most 64 MiB of HBM per device.

```python
import jax
import jax.numpy as jnp

ORBS = 512
COLS = 1024
SLICES = 4
LEVELS = 2


def identity_blocks(key):
    noise_key = jax.random.fold_in(key, 1)
    diag_key = jax.random.fold_in(key, 2)
    noise = jnp.clip(jax.random.normal(noise_key, (2, SLICES, ORBS, ORBS), jnp.float32), -4.0, 4.0)
    noise = noise / -jnp.min(noise) * 0.078125
    unit_matrix = jnp.eye(ORBS, dtype=jnp.float32)
    raw_diag = jax.random.uniform(diag_key, (SLICES, ORBS), jnp.float32, 0.0, 1.0)
    lowest = jnp.min(raw_diag)
    highest = jnp.max(raw_diag)
    shifted = (raw_diag - lowest) / (highest - lowest)
    diag_part = 0.125 * (2.0 * shifted - 1.0)
    real_part = noise[0] * (1.0 - unit_matrix) + unit_matrix * (1.0 + diag_part[:, :, None])
    return jnp.stack([real_part, noise[1]]).astype(jnp.bfloat16)


def draw_dinv(key, part):
    return identity_blocks(jax.random.fold_in(key, 11))


def draw_merge_inv(key, part):
    return identity_blocks(jax.random.fold_in(key, 23))


def block_scale(key, dims, shards, smallest, high):
    level, own = 1.0, jax.random.fold_in(key, 6)
    for dim, parts in shards:
        draws = jnp.exp(jax.random.uniform(jax.random.fold_in(own, dim), (parts,), jnp.float32, smallest / len(shards), high / len(shards)))
        level = level * jnp.repeat(draws, dims[dim] // parts).reshape([-1 if axis == dim else 1 for axis in range(len(dims))])
    return level


def centred(key, extent, scale, reach, shards=(), held_as=jnp.bfloat16):
    values = jax.random.normal(key, extent, jnp.float32) * scale
    if len(shards) > 0:
        values = block_scale(key, extent, shards, -0.22, 0.18) * values
    return jnp.clip(values, min=-reach, max=reach).astype(held_as)


def setup_inputs(seed: int = 0, part: int = 0) -> dict:
    arg_keys = jax.random.split(jax.random.key(seed), 5)
    part_keys = jax.random.split(jax.random.fold_in(arg_keys[4], part), 5)
    rhs = centred(part_keys[0], (2, SLICES, ORBS, COLS), 1.0, 6.0, ((1, 4), (3, 4)))
    dinv = draw_dinv(jax.random.fold_in(jax.random.fold_in(arg_keys[4], part), 71), part)
    spikes = centred(part_keys[2], (2, SLICES, LEVELS, ORBS, ORBS), (8 * ORBS) ** -0.5, 0.09375, ((1, 4), (3, 2)))
    merge_inv = draw_merge_inv(jax.random.fold_in(jax.random.fold_in(arg_keys[4], part), 71), part)
    return {"rhs": rhs, "dinv": dinv, "spikes": spikes, "merge_inv": merge_inv}


def complex_product(matrix, operand):
    matrix = matrix.astype(jnp.float32)
    operand = operand.astype(jnp.float32)
    real_part = jnp.einsum("...ij,...jk->...ik", matrix[0], operand[0]) - jnp.einsum("...ij,...jk->...ik", matrix[1], operand[1])
    imag_part = jnp.einsum("...ij,...jk->...ik", matrix[0], operand[1]) + jnp.einsum("...ij,...jk->...ik", matrix[1], operand[0])
    return jnp.stack([real_part, imag_part])


def reference(rhs, dinv, spikes, merge_inv):
    current = complex_product(dinv, rhs)
    for height in range(LEVELS):
        half_span = 2 ** height
        groups = SLICES // (2 * half_span)
        shaped = current.reshape(2, groups, 2 * half_span, ORBS, COLS)
        rounded = shaped.astype(jnp.bfloat16)
        spike_now = spikes[:, :, height].reshape(2, groups, 2 * half_span, ORBS, ORBS)
        merge_now = merge_inv.reshape(2, groups, 2 * half_span, ORBS, ORBS)[:, :, half_span - 1]
        interior = shaped[:, :, half_span - 1] - complex_product(spike_now[:, :, half_span - 1], rounded[:, :, half_span])
        left_tip = complex_product(merge_now, interior.astype(jnp.bfloat16)).astype(jnp.bfloat16)
        spread_left = jnp.broadcast_to(left_tip[:, :, None], (2, groups, half_span, ORBS, COLS))
        right_part = shaped[:, :, half_span:] - complex_product(spike_now[:, :, half_span:], spread_left)
        right_tip = right_part[:, :, 0].astype(jnp.bfloat16)
        spread_right = jnp.broadcast_to(right_tip[:, :, None], (2, groups, half_span, ORBS, COLS))
        left_part = shaped[:, :, :half_span] - complex_product(spike_now[:, :, :half_span], spread_right)
        current = jnp.concatenate([left_part, right_part], axis=2).reshape(2, SLICES, ORBS, COLS)
    return current
```

```python
import functools

import jax
import jax.numpy as jnp
from jax import lax
from jax.experimental import pallas as pl
from jax.experimental.pallas import tpu as pltpu
from jax.sharding import PartitionSpec as P

VMEM = pl.BlockSpec(memory_space=pltpu.VMEM)


def ring_gather(block, axis):
    count = lax.axis_size(axis)
    blocks = [block]
    for step in range(1, count):
        blocks.append(lax.ppermute(block, axis, [((i + step) % count, i) for i in range(count)]))
    return blocks


def row_starts(height, orb_count, col_parts):
    orb = lax.axis_index("orb")
    per_orb = height // orb_count
    starts = []
    for j in range(orb_count):
        base = lax.rem(orb + j, orb_count) * per_orb
        if col_parts == 1:
            starts.append(base)
            continue
        col = lax.axis_index("col")
        for k in range(col_parts):
            starts.append(base + lax.rem(col + k, col_parts) * (per_orb // col_parts))
    return starts


def rows_of(start, size):
    return pl.ds(pl.multiple_of(start, size), size)


def turned(field):
    half = field.shape[1] // 2
    return jnp.concatenate([-field[:, half:], field[:, :half]], axis=1)


def each_product(pieces, starts, field):
    field_i = turned(field)
    for piece, start in zip(pieces, starts):
        real, imag = piece[0], piece[1]
        yield (
            rows_of(start, real.shape[0]),
            jnp.dot(real, field, preferred_element_type=jnp.float32)
            + jnp.dot(imag, field_i, preferred_element_type=jnp.float32),
        )


def call(body, outs, scratch, *args, flops=0, aliases=None):
    nbytes = sum(a.size * a.dtype.itemsize for a in args) + sum(o.size * o.dtype.itemsize for o in outs)
    return pl.pallas_call(
        body,
        out_shape=outs,
        in_specs=[VMEM] * len(args),
        out_specs=[VMEM] * len(outs),
        scratch_shapes=scratch,
        compiler_params=pltpu.CompilerParams(vmem_limit_bytes=24 * 2**20),
        cost_estimate=pl.CostEstimate(flops=flops, bytes_accessed=nbytes, transcendentals=0),
    )(*args)


def product_flops(height, width):
    return 2 * 2 * height * height * width


def start_state(pieces, rhs, chunks):
    height, columns = rhs.shape[1:]
    part = columns // chunks
    orb_count = len(pieces)

    def body(*refs):
        mats, rhs_ref, outs = refs[:orb_count], refs[orb_count], refs[orb_count + 1 :]
        starts = row_starts(height, orb_count, 1)
        for c in range(chunks):
            window = pl.ds(c * part, part)
            field = jnp.concatenate([rhs_ref[0, :, window], rhs_ref[1, :, window]], axis=1)
            for rows, value in each_product(mats, starts, field):
                outs[2 * c][rows, :] = value
                outs[2 * c + 1][rows, :] = value.astype(jnp.bfloat16)

    shape = (height, 2 * part)
    outs = [jax.ShapeDtypeStruct(shape, t) for _ in range(chunks) for t in (jnp.float32, jnp.bfloat16)]
    flat = call(body, outs, [], *pieces, rhs, flops=chunks * product_flops(height, 2 * part))
    return flat[0::2], flat[1::2]


def left_tip(is_left, state, hb_next, spike, merge):
    height, width = state.shape
    n = len(spike)

    def body(*refs):
        state_ref, hb_ref = refs[:2]
        spike_refs, merge_refs = refs[2 : 2 + n], refs[2 + n : 2 + 2 * n]
        out, inner = refs[2 + 2 * n :]
        starts = row_starts(height, n, 1)

        @pl.when(is_left())
        def _():
            for rows, value in each_product(spike_refs, starts, hb_ref[...]):
                inner[rows, :] = (state_ref[rows, :] - value).astype(jnp.bfloat16)
            for rows, value in each_product(merge_refs, starts, inner[...]):
                out[rows, :] = value.astype(jnp.bfloat16)

    (zl,) = call(
        body,
        [jax.ShapeDtypeStruct((height, width), jnp.bfloat16)],
        [pltpu.VMEM((height, width), jnp.bfloat16)],
        state, hb_next, *spike, *merge,
        flops=2 * product_flops(height, width),
    )
    return zl


def left_update(is_left, state, hb_next, zl, spike, spike_next):
    height, width = state.shape
    n, m = len(spike), len(spike_next)

    def body(*refs):
        state_ref, hb_ref, zl_ref = refs[:3]
        spike_refs, next_refs = refs[3 : 3 + n], refs[3 + n : 3 + n + m]
        out, out_b, inner = refs[3 + n + m :]

        @pl.when(is_left())
        def _():
            for rows, value in each_product(next_refs, row_starts(height, n, m // n), zl_ref[...]):
                inner[rows, :] = (hb_ref[rows, :].astype(jnp.float32) - value).astype(jnp.bfloat16)
            for rows, value in each_product(spike_refs, row_starts(height, n, 1), inner[...]):
                new = state_ref[rows, :] - value
                out[rows, :] = new
                out_b[rows, :] = new.astype(jnp.bfloat16)

        @pl.when(jnp.logical_not(is_left()))
        def _():
            out[...] = state_ref[...]
            out_b[...] = state_ref[...].astype(jnp.bfloat16)

    return call(
        body,
        [jax.ShapeDtypeStruct((height, width), t) for t in (jnp.float32, jnp.bfloat16)],
        [pltpu.VMEM((height, width), jnp.bfloat16)],
        state, hb_next, zl, *spike, *spike_next,
        flops=2 * product_flops(height, width),
    )


def right_update(is_right, state, zl, spike):
    height, width = state.shape
    n = len(spike)

    def body(*refs):
        state_ref, zl_ref = refs[:2]
        spike_refs, (out,) = refs[2 : 2 + n], refs[2 + n :]

        @pl.when(is_right())
        def _():
            for rows, value in each_product(spike_refs, row_starts(height, n, 1), zl_ref[...]):
                out[rows, :] = state_ref[rows, :] - value

        @pl.when(jnp.logical_not(is_right()))
        def _():
            out[...] = state_ref[...]

    (new,) = call(
        body,
        [jax.ShapeDtypeStruct((height, width), jnp.float32)],
        [],
        state, zl, *spike,
        flops=product_flops(height, width),
    )
    return new


def tip_of(is_left, hb_next, zl, arrived, spike_next, orb_count):
    height, width = zl.shape
    m = len(spike_next)

    def body(*refs):
        hb_ref, zl_ref, arrived_ref = refs[:3]
        next_refs, (out,) = refs[3 : 3 + m], refs[3 + m :]

        @pl.when(is_left())
        def _():
            starts = row_starts(height, orb_count, m // orb_count)
            for rows, value in each_product(next_refs, starts, zl_ref[...]):
                out[rows, :] = (hb_ref[rows, :].astype(jnp.float32) - value).astype(jnp.bfloat16)

        @pl.when(jnp.logical_not(is_left()))
        def _():
            out[...] = arrived_ref[...]

    (tip,) = call(
        body,
        [jax.ShapeDtypeStruct((height, width), jnp.bfloat16)],
        [],
        hb_next, zl, arrived, *spike_next,
        flops=product_flops(height, width),
    )
    return tip


def pick(use_new, new, old):
    def body(new_ref, old_ref, out):
        @pl.when(use_new())
        def _():
            out[...] = new_ref[...]

        @pl.when(jnp.logical_not(use_new()))
        def _():
            out[...] = old_ref[...]

    (out,) = call(body, [jax.ShapeDtypeStruct(old.shape, old.dtype)], [], new, old)
    return out


def tip_update(use_new, state, new_tip, tip, spike):
    height, width = state.shape
    n = len(spike)

    def body(*refs):
        state_ref, new_ref, tip_ref = refs[:3]
        spike_refs, (out, out_b) = refs[3 : 3 + n], refs[3 + n :]

        def update(source):
            for rows, value in each_product(spike_refs, row_starts(height, n, 1), source[...]):
                new = state_ref[rows, :] - value
                out[rows, :] = new
                out_b[rows, :] = new.astype(jnp.bfloat16)

        @pl.when(use_new())
        def _():
            update(new_ref)

        @pl.when(jnp.logical_not(use_new()))
        def _():
            update(tip_ref)

    return call(
        body,
        [jax.ShapeDtypeStruct((height, width), t) for t in (jnp.float32, jnp.bfloat16)],
        [],
        state, new_tip, tip, *spike,
        flops=product_flops(height, width),
    )


def per_device(chunks, rhs, dinv, spikes, merge_inv):
    slabs = lax.axis_size("slab")
    cols = lax.axis_size("col")
    orb_count = lax.axis_size("orb")
    levels = spikes.shape[2]
    height = dinv.shape[3]
    device = lax.axis_index("slab")

    level_of = jnp.int32(0)
    for level in range(1, levels):
        level_of = jnp.where(lax.rem(device, 1 << level) == 0, level, level_of)
    part = height // orb_count // cols
    mine = lax.dynamic_slice(
        spikes,
        (0, 0, level_of, lax.axis_index("col") * part, 0),
        (2, 1, 1, part, height),
    ).reshape(2, part, height)
    backward = [(i, i - 1) for i in range(1, slabs)]
    quarter = lax.ppermute(mine, "slab", backward)

    inverse = ring_gather(dinv[:, 0], "orb")
    states, hbs = start_state(inverse, rhs[:, 0], chunks)
    states, hbs = list(states), list(hbs)
    spike_all = [ring_gather(spikes[:, 0, level], "orb") for level in range(levels)]
    merge = ring_gather(merge_inv[:, 0], "orb")
    spike_next = []
    for piece in ring_gather(quarter, "col"):
        spike_next.append(ring_gather(piece, "orb"))
    spike_next = [spike_next[k][j] for j in range(orb_count) for k in range(cols)]

    early = hbs
    for level in range(levels):
        span = 1 << level
        heads = range(0, slabs, 2 * span)
        spike = spike_all[level]

        def position(span=span):
            return lax.rem(lax.axis_index("slab"), 2 * span)

        def is_left(span=span, position=position):
            return position() == span - 1

        def is_right(span=span, position=position):
            return position() >= span

        down = [(g + span, g + span - 1) for g in heads]
        up = [(g + span - 1, g + span) for g in heads]
        hb_next = [lax.ppermute(early[c], "slab", down) for c in range(chunks)]
        zl = [left_tip(is_left, states[c], hb_next[c], spike, merge) for c in range(chunks)]
        arrived = [lax.ppermute(zl[c], "slab", up) for c in range(chunks)]
        if span == 1:
            for c in range(chunks):
                states[c], hbs[c] = left_update(is_left, states[c], hb_next[c], zl[c], spike, spike_next)
                early = list(hbs)
            for c in range(chunks):
                states[c] = right_update(is_right, states[c], arrived[c], spike)
            continue
        tips = [tip_of(is_left, hb_next[c], zl[c], arrived[c], spike_next, orb_count) for c in range(chunks)]
        reach = 1
        while reach < span:
            route = []
            for g in heads:
                for j in range(reach):
                    if j + reach < span:
                        route.append((g + span + j, g + span + j + reach))
                        route.append((g + span - 1 - j, g + span - 1 - j - reach))
            moved = [lax.ppermute(tips[c], "slab", route) for c in range(chunks)]

            def is_new(span=span, position=position, reach=reach):
                far = jnp.where(position() >= span, position() - span, span - 1 - position())
                return jnp.logical_and(far >= reach, far < 2 * reach)

            if 2 * reach < span:
                tips = [pick(is_new, moved[c], tips[c]) for c in range(chunks)]
            reach *= 2
        for c in range(chunks):
            states[c], hbs[c] = tip_update(is_new, states[c], moved[c], tips[c], spike)
        early = list(hbs)

    half = [s.shape[1] // 2 for s in states]
    real = jnp.concatenate([s[:, :h] for s, h in zip(states, half)], axis=1)
    imag = jnp.concatenate([s[:, h:] for s, h in zip(states, half)], axis=1)
    return jnp.stack([real, imag])[:, None]


def solution(mesh):
    placed = (
        P(None, ("energy", "slab"), None, ("col", "orb")),
        P(None, ("energy", "slab"), "orb", None),
        P(None, ("energy", "slab"), None, "orb", None),
        P(None, ("energy", "slab"), "orb", None),
    )

    def body(rhs, dinv, spikes, merge_inv):
        chunks = 2 if rhs.shape[3] % 256 == 0 else 1
        return per_device(chunks, rhs, dinv, spikes, merge_inv)

    return jax.shard_map(
        body,
        mesh=mesh,
        in_specs=placed,
        out_specs=P(None, ("energy", "slab"), None, ("col", "orb")),
        check_vma=False,
    )
```

```python
import jax
import jax.numpy as jnp
from jax import lax
from jax.experimental import pallas as pl
from jax.experimental.pallas import tpu as pltpu
from jax.sharding import PartitionSpec as P

VMEM = pl.BlockSpec(memory_space=pltpu.VMEM)
SHARES = (1, 1)


def ring_gather(block, axis):
    count = lax.axis_size(axis)
    blocks = [block]
    for step in range(1, count):
        blocks.append(lax.ppermute(block, axis, [((i + step) % count, i) for i in range(count)]))
    return blocks


def row_starts(height, orb_count, col_parts):
    orb = lax.axis_index("orb")
    per_orb = height // orb_count
    starts = []
    for j in range(orb_count):
        base = lax.rem(orb + j, orb_count) * per_orb
        if col_parts == 1:
            starts.append(base)
            continue
        col = lax.axis_index("col")
        for k in range(col_parts):
            starts.append(base + lax.rem(col + k, col_parts) * (per_orb // col_parts))
    return starts


def rows_of(start, size):
    return pl.ds(pl.multiple_of(start, size), size)


def turned(field):
    half = field.shape[1] // 2
    return jnp.concatenate([-field[:, half:], field[:, :half]], axis=1)


def at_level(spikes, level):
    return [tuple(lambda s=s, p=p: s[p, level] for p in range(2)) for s in spikes]


def parts_of(pieces):
    return [tuple(lambda m=m, p=p: m[p] for p in range(2)) for m in pieces]


def packed(refs, height, width):
    blocks = height // width
    size = (refs[0].shape[0] - height) // (2 * blocks)

    def load(ref, part):
        first = height + part * blocks * size
        return jnp.concatenate([ref[pl.ds(first + k * size, size), :] for k in range(blocks)], axis=1)

    return [tuple(lambda r=r, p=p: load(r, p) for p in range(2)) for r in refs]


def each_product(pieces, starts, field):
    field_i = turned(field)
    for (real, imag), start in zip(pieces, starts):
        value = jnp.dot(real(), field, preferred_element_type=jnp.float32)
        value += jnp.dot(imag(), field_i, preferred_element_type=jnp.float32)
        yield rows_of(start, value.shape[0]), value


def call(body, outs, scratch, *args, flops=0, aliases=None):
    nbytes = sum(a.size * a.dtype.itemsize for a in args) + sum(o.size * o.dtype.itemsize for o in outs)
    return pl.pallas_call(
        body,
        out_shape=outs,
        in_specs=[VMEM] * len(args),
        out_specs=[VMEM] * len(outs),
        scratch_shapes=scratch,
        compiler_params=pltpu.CompilerParams(vmem_limit_bytes=24 * 2**20),
        cost_estimate=pl.CostEstimate(flops=flops, bytes_accessed=nbytes, transcendentals=0),
    )(*args)


def product_flops(height, width):
    return 2 * 2 * height * height * width


def is_even():
    return lax.rem(lax.axis_index("slab"), 2) == 0


def lowest_bit(number, levels):
    found = jnp.int32(0)
    for level in range(1, levels):
        found = jnp.where(lax.rem(number, 1 << level) == 0, level, found)
    return found


def start_state(pieces, rhs, first, width):
    height = rhs.shape[1]
    n = len(pieces)

    def body(*refs):
        mats, rhs_ref, (out, out_b) = refs[:n], refs[n], refs[n + 1 :]
        window = pl.ds(first, width)
        field = jnp.concatenate([rhs_ref[0, :, window], rhs_ref[1, :, window]], axis=1)
        for rows, value in each_product(parts_of(mats), row_starts(height, n, 1), field):
            out[rows, :] = value
            out_b[rows, :] = value.astype(jnp.bfloat16)

    outs = [jax.ShapeDtypeStruct((height, 2 * width), t) for t in (jnp.float32, jnp.bfloat16)]
    return call(body, outs, [], *pieces, rhs, flops=product_flops(height, 2 * width))


def send_field(odd_sends_product, merge_refs, height, hb_ref, store):
    n = len(merge_refs)
    left = jnp.logical_xor(is_even(), odd_sends_product)

    @pl.when(left)
    def _():
        for rows, value in each_product(parts_of(merge_refs), row_starts(height, n, 1), hb_ref[...]):
            store(rows, value.astype(jnp.bfloat16))

    @pl.when(jnp.logical_not(left))
    def _():
        store(pl.ds(0, height), hb_ref[...])


def first_sends(spikes, merge, hb, levels):
    height, width = hb.shape
    n = len(spikes)
    size = height // n
    blocks = height // width
    cut = min(128, width)

    def body(*refs):
        spike_refs, merge_refs, hb_ref = refs[:n], refs[n : 2 * n], refs[2 * n]
        q_out, pay, later = refs[2 * n + 1 :]
        device = lax.axis_index("slab")
        level_left = lowest_bit(device + 1, levels)
        level_right = lowest_bit(device, levels)
        starts = row_starts(height, n, 1)

        def columns(k, carry):
            window = pl.ds(pl.multiple_of(k * cut, cut), cut)
            order = [jnp.concatenate([s[p, level_left, :, window] for s in spike_refs], axis=0) for p in range(2)]
            if n > 1:
                first = lax.axis_index("orb")
                order = [in_place(x, first, n) for x in order]
            field = jnp.concatenate(order, axis=1)
            for _, value in each_product(parts_of(merge_refs[:1]), starts[:1], field):
                q_out[0, :, window] = value[:, :cut].astype(jnp.bfloat16)
                q_out[1, :, window] = value[:, cut:].astype(jnp.bfloat16)
            return carry

        lax.fori_loop(0, height // cut, columns, 0)

        def pack(source):
            for p in range(2):
                for k in range(blocks):
                    pay[pl.ds(height + (p * blocks + k) * size, size), :] = source(p, pl.ds(k * width, width))

        @pl.when(is_even())
        def _():
            pack(lambda p, window: q_out[p, :, window])
            for p in range(2):
                later[p] = spike_refs[0][p, level_right]

        @pl.when(jnp.logical_not(is_even()))
        def _():
            pack(lambda p, window: spike_refs[0][p, 0, :, window])
            later[...] = q_out[...]

        def store(rows, value):
            pay[rows, :] = value

        send_field(False, merge_refs, height, hb_ref, store)

    return call(
        body,
        [
            jax.ShapeDtypeStruct((2, size, height), jnp.bfloat16),
            jax.ShapeDtypeStruct((height + 2 * blocks * size, width), jnp.bfloat16),
            jax.ShapeDtypeStruct((2, size, height), jnp.bfloat16),
        ],
        [],
        *spikes, *merge, hb,
        flops=2 * product_flops(height, width),
    )


def in_place(rows, first, count):
    size = rows.shape[0] // count
    out = rows
    for shift in range(1, count):
        rolled = jnp.concatenate([rows[rows.shape[0] - shift * size :], rows[: rows.shape[0] - shift * size]], axis=0)
        out = jnp.where(first == shift, rolled, out)
    return out


def next_sends(merge, hb):
    height, width = hb.shape
    n = len(merge)

    def body(*refs):
        merge_refs, hb_ref, out = refs[:n], refs[n], refs[n + 1]

        def store(rows, value):
            out[rows, :] = value

        send_field(False, merge_refs, height, hb_ref, store)

    (out,) = call(
        body, [jax.ShapeDtypeStruct(hb.shape, jnp.bfloat16)], [], *merge, hb, flops=product_flops(height, width)
    )
    return out


def merge_tip(left, q_refs, mats, height, mine, got, source, store):
    n = len(q_refs)
    starts = row_starts(height, n, 1)

    @pl.when(left)
    def _():
        for rows, value in each_product(parts_of(q_refs), starts, got[pl.ds(0, height), :]):
            source[rows, :] = (mine[rows, :].astype(jnp.float32) - value).astype(jnp.bfloat16)

    @pl.when(jnp.logical_not(left))
    def _():
        source[...] = mine[pl.ds(0, height), :]

    for rows, value in each_product(mats, starts, source[...]):
        store(rows, (got[rows, :].astype(jnp.float32) - value).astype(jnp.bfloat16))


def first_level(state, mine, got, payloads, q, spikes, merge):
    height, width = state.shape
    n = len(q)

    def body(*refs):
        state_ref, mine_ref, got_ref = refs[:3]
        pay_refs, q_refs, spike_refs, merge_refs = (refs[3 + k * n : 3 + (k + 1) * n] for k in range(4))
        out, send, source, tip = refs[3 + 4 * n :]

        def store_tip(rows, value):
            tip[rows, :] = value

        merge_tip(is_even(), q_refs, packed(pay_refs, height, width), height, mine_ref, got_ref, source, store_tip)
        for rows, value in each_product(at_level(spike_refs, 0), row_starts(height, n, 1), tip[...]):
            new = state_ref[rows, :] - value
            out[rows, :] = new
            source[rows, :] = new.astype(jnp.bfloat16)

        def store(rows, value):
            send[rows, :] = value

        send_field(True, merge_refs, height, source, store)

    return call(
        body,
        [jax.ShapeDtypeStruct((height, width), t) for t in (jnp.float32, jnp.bfloat16)],
        [pltpu.VMEM((height, width), jnp.bfloat16)] * 2,
        state, mine, got, *payloads, *q, *spikes, *merge,
        flops=4 * product_flops(height, width),
    )


def later_tip(position, span, mine, got, mats, q):
    height, width = mine.shape
    n = len(q)

    def body(*refs):
        mine_ref, got_ref = refs[:2]
        mat_refs, q_refs = refs[2 : 2 + n], refs[2 + n : 2 + 2 * n]
        out, source = refs[2 + 2 * n :]
        place = position()

        def store(rows, value):
            out[rows, :] = value

        @pl.when(jnp.logical_or(place == span - 1, place == span))
        def _():
            merge_tip(place == span - 1, q_refs, parts_of(mat_refs), height, mine_ref, got_ref, source, store)

    (tip,) = call(
        body,
        [jax.ShapeDtypeStruct((height, width), jnp.bfloat16)],
        [pltpu.VMEM((height, width), jnp.bfloat16)],
        mine, got, *mats, *q,
        flops=2 * product_flops(height, width),
    )
    return tip


def pick(use_new, new, old):
    def body(new_ref, old_ref, out):
        @pl.when(use_new())
        def _():
            out[...] = new_ref[...]

        @pl.when(jnp.logical_not(use_new()))
        def _():
            out[...] = old_ref[...]

    (out,) = call(body, [jax.ShapeDtypeStruct(old.shape, old.dtype)], [], new, old)
    return out


def tip_update(use_new, state, new_tip, tip, spikes, level, merge=()):
    height, width = state.shape
    n = len(spikes)
    kinds = (jnp.float32, jnp.bfloat16) if merge else (jnp.float32,)

    def body(*refs):
        state_ref, new_ref, tip_ref = refs[:3]
        spike_refs, merge_refs = refs[3 : 3 + n], refs[3 + n : 3 + n + len(merge)]
        outs, source = refs[3 + n + len(merge) : -1], refs[-1]

        @pl.when(use_new())
        def _():
            source[...] = new_ref[...]

        @pl.when(jnp.logical_not(use_new()))
        def _():
            source[...] = tip_ref[...]

        starts = row_starts(height, n, 1)
        for rows, value in each_product(at_level(spike_refs, level), starts, source[...]):
            outs[0][rows, :] = state_ref[rows, :] - value
        if not merge:
            return
        source[...] = outs[0][...].astype(jnp.bfloat16)

        def store(rows, value):
            outs[1][rows, :] = value

        send_field(True, merge_refs, height, source, store)

    return call(
        body,
        [jax.ShapeDtypeStruct((height, width), t) for t in kinds],
        [pltpu.VMEM((height, width), jnp.bfloat16)],
        state, new_tip, tip, *spikes, *merge,
        flops=product_flops(height, width),
    )


def last_update(use_new, done, state, new_tip, tip, spikes, level):
    height, width = state.shape
    n, k = len(spikes), len(done)
    own = width // 2
    before = sum(d.shape[1] // 2 for d in done)
    columns = before + own
    split = before - before % 128

    def body(*refs):
        done_refs = refs[:k]
        state_ref, new_ref, tip_ref = refs[k : k + 3]
        spike_refs = refs[k + 3 : k + 3 + n]
        out, source, whole, sems = refs[k + 3 + n :]

        first = 0
        for d in done_refs:
            w = d.shape[1] // 2
            whole[0, :, pl.ds(first, w)] = d[:, :w]
            whole[1, :, pl.ds(first, w)] = d[:, w:]
            first += w
        copies = []
        if split:
            window = pl.ds(0, split)
            copies.append(pltpu.make_async_copy(whole.at[:, :, window], out.at[:, :, window], sems.at[0]))
            copies[0].start()

        @pl.when(use_new())
        def _():
            source[...] = new_ref[...]

        @pl.when(jnp.logical_not(use_new()))
        def _():
            source[...] = tip_ref[...]

        starts = row_starts(height, n, 1)
        for rows, value in each_product(at_level(spike_refs, level), starts, source[...]):
            new = state_ref[rows, :] - value
            whole[0, rows, pl.ds(before, own)] = new[:, :own]
            whole[1, rows, pl.ds(before, own)] = new[:, own:]
        window = pl.ds(split, columns - split)
        copies.append(pltpu.make_async_copy(whole.at[:, :, window], out.at[:, :, window], sems.at[1]))
        copies[-1].start()
        for copy in copies:
            copy.wait()

    return pl.pallas_call(
        body,
        out_shape=jax.ShapeDtypeStruct((2, height, columns), jnp.float32),
        in_specs=[VMEM] * (k + 3 + n),
        out_specs=pl.BlockSpec(memory_space=pl.ANY),
        scratch_shapes=[
            pltpu.VMEM((height, width), jnp.bfloat16),
            pltpu.VMEM((2, height, columns), jnp.float32),
            pltpu.SemaphoreType.DMA((2,)),
        ],
        compiler_params=pltpu.CompilerParams(vmem_limit_bytes=24 * 2**20),
        cost_estimate=pl.CostEstimate(
            flops=product_flops(height, width), bytes_accessed=12 * height * columns, transcendentals=0
        ),
    )(*done, state, new_tip, tip, *spikes)


def swap(block, pairs):
    return lax.ppermute(block, "slab", pairs + [(b, a) for a, b in pairs])


def per_device(widths, rhs, dinv, spikes, merge_inv):
    slabs = lax.axis_size("slab")
    levels = spikes.shape[2]
    chunks = range(len(widths))

    inverse = ring_gather(dinv[:, 0], "orb")
    spike_all = ring_gather(spikes[:, 0], "orb")
    merge = ring_gather(merge_inv[:, 0], "orb")
    states, hbs = [], []
    for c in chunks:
        state, hb = start_state(inverse, rhs[:, 0], sum(widths[:c]), widths[c])
        states.append(state)
        hbs.append(hb)

    q_own, pay, later = first_sends(spike_all, merge, hbs[0], levels)
    pairs = [(i, i + 1) for i in range(0, slabs, 2)]
    pay_got = swap(pay, pairs)
    mats = ring_gather(swap(later, [(i, i + 1) for i in range(1, slabs - 1, 2)]), "orb")
    q = ring_gather(q_own, "orb")
    sends = [pay] + [next_sends(merge, hbs[c]) for c in chunks[1:]]
    gots = [pay_got] + [swap(sends[c], pairs) for c in chunks[1:]]
    payloads = ring_gather(pay_got, "orb")
    for c in chunks:
        states[c], sends[c] = first_level(states[c], sends[c], gots[c], payloads, q, spike_all, merge)

    for level in range(1, levels):
        span = 1 << level
        heads = range(0, slabs, 2 * span)

        def position(span=span):
            return lax.rem(lax.axis_index("slab"), 2 * span)

        gots = [swap(sends[c], [(g + span - 1, g + span) for g in heads]) for c in chunks]
        tips = [later_tip(position, span, sends[c], gots[c], mats, q) for c in chunks]
        reach = 1
        while reach < span:
            route = []
            for g in heads:
                for j in range(reach):
                    if j + reach < span:
                        route.append((g + span + j, g + span + j + reach))
                        route.append((g + span - 1 - j, g + span - 1 - j - reach))
            moved = [lax.ppermute(tips[c], "slab", route) for c in chunks]

            def is_new(span=span, position=position, reach=reach):
                far = jnp.where(position() >= span, position() - span, span - 1 - position())
                return jnp.logical_and(far >= reach, far < 2 * reach)

            if 2 * reach < span:
                tips = [pick(is_new, moved[c], tips[c]) for c in chunks]
            reach *= 2
        if level < levels - 1:
            for c in chunks:
                states[c], sends[c] = tip_update(is_new, states[c], moved[c], tips[c], spike_all, level, merge)
            continue
        for c in chunks[:-1]:
            (states[c],) = tip_update(is_new, states[c], moved[c], tips[c], spike_all, level)
        c = chunks[-1]
        whole = last_update(is_new, states[:c], states[c], moved[c], tips[c], spike_all, level)
    return whole[:, None]


def chunk_widths(columns):
    total = sum(SHARES)
    if columns * min(SHARES) // total < 64:
        return [columns]
    return [columns * s // total for s in SHARES]


def solution(mesh):
    placed = (
        P(None, ("energy", "slab"), None, ("col", "orb")),
        P(None, ("energy", "slab"), "orb", None),
        P(None, ("energy", "slab"), None, "orb", None),
        P(None, ("energy", "slab"), "orb", None),
    )

    def body(rhs, dinv, spikes, merge_inv):
        return per_device(chunk_widths(rhs.shape[3]), rhs, dinv, spikes, merge_inv)

    return jax.shard_map(
        body,
        mesh=mesh,
        in_specs=placed,
        out_specs=P(None, ("energy", "slab"), None, ("col", "orb")),
        check_vma=False,
    )
```

```python
import jax
import jax.numpy as jnp
from jax import lax
from jax.experimental import pallas as pl
from jax.experimental.pallas import tpu as pltpu
from jax.sharding import PartitionSpec as P

VMEM = pl.BlockSpec(memory_space=pltpu.VMEM)
SHARES = (1, 1)


def ring_gather(block, axis):
    count = lax.axis_size(axis)
    blocks = [block]
    for step in range(1, count):
        blocks.append(lax.ppermute(block, axis, [((i + step) % count, i) for i in range(count)]))
    return blocks


def row_starts(height, orb_count, col_parts):
    orb = lax.axis_index("orb")
    per_orb = height // orb_count
    starts = []
    for j in range(orb_count):
        base = lax.rem(orb + j, orb_count) * per_orb
        if col_parts == 1:
            starts.append(base)
            continue
        col = lax.axis_index("col")
        for k in range(col_parts):
            starts.append(base + lax.rem(col + k, col_parts) * (per_orb // col_parts))
    return starts


def rows_of(start, size):
    return pl.ds(pl.multiple_of(start, size), size)


def turned(field):
    half = field.shape[1] // 2
    return jnp.concatenate([-field[:, half:], field[:, :half]], axis=1)


def at_level(spikes, level):
    return [tuple(lambda s=s, p=p: s[p, level] for p in range(2)) for s in spikes]


def parts_of(pieces):
    return [tuple(lambda m=m, p=p: m[p] for p in range(2)) for m in pieces]


def each_product(pieces, starts, field):
    field_i = turned(field)
    for (real, imag), start in zip(pieces, starts):
        value = jnp.dot(real(), field, preferred_element_type=jnp.float32)
        value += jnp.dot(imag(), field_i, preferred_element_type=jnp.float32)
        yield rows_of(start, value.shape[0]), value


def call(body, outs, scratch, *args, flops=0, aliases=None):
    nbytes = sum(a.size * a.dtype.itemsize for a in args) + sum(o.size * o.dtype.itemsize for o in outs)
    return pl.pallas_call(
        body,
        out_shape=outs,
        in_specs=[VMEM] * len(args),
        out_specs=[VMEM] * len(outs),
        scratch_shapes=scratch,
        compiler_params=pltpu.CompilerParams(vmem_limit_bytes=24 * 2**20),
        cost_estimate=pl.CostEstimate(flops=flops, bytes_accessed=nbytes, transcendentals=0),
    )(*args)


def product_flops(height, width):
    return 2 * 2 * height * height * width


def is_even():
    return lax.rem(lax.axis_index("slab"), 2) == 0


def lowest_bit(number, levels):
    found = jnp.int32(0)
    for level in range(1, levels):
        found = jnp.where(lax.rem(number, 1 << level) == 0, level, found)
    return found


def fetch(*arrays):
    n = len(arrays)

    def body(*refs):
        sems = refs[-1]
        copies = [pltpu.make_async_copy(refs[k], refs[n + k], sems.at[k]) for k in range(n)]
        for copy in copies:
            copy.start()
        for copy in copies:
            copy.wait()

    return pl.pallas_call(
        body,
        out_shape=[jax.ShapeDtypeStruct(a.shape, a.dtype) for a in arrays],
        in_specs=[pl.BlockSpec(memory_space=pl.ANY)] * n,
        out_specs=[VMEM] * n,
        scratch_shapes=[pltpu.SemaphoreType.DMA((n,))],
        compiler_params=pltpu.CompilerParams(vmem_limit_bytes=48 * 2**20),
        cost_estimate=pl.CostEstimate(flops=0, bytes_accessed=2 * sum(a.size * 2 for a in arrays), transcendentals=0),
    )(*arrays)


def start_state(pieces, rhs, first, width):
    height = rhs.shape[1]
    n = len(pieces)

    def body(*refs):
        mats, rhs_ref, (out, out_b) = refs[:n], refs[n], refs[n + 1 :]
        window = pl.ds(first, width)
        field = jnp.concatenate([rhs_ref[0, :, window], rhs_ref[1, :, window]], axis=1)
        for rows, value in each_product(parts_of(mats), row_starts(height, n, 1), field):
            out[rows, :] = value
            out_b[rows, :] = value.astype(jnp.bfloat16)

    outs = [jax.ShapeDtypeStruct((height, 2 * width), t) for t in (jnp.float32, jnp.bfloat16)]
    return call(body, outs, [], *pieces, rhs, flops=product_flops(height, 2 * width))


def send_field(odd_sends_product, merge_refs, height, hb_ref, store):
    n = len(merge_refs)
    left = jnp.logical_xor(is_even(), odd_sends_product)

    @pl.when(left)
    def _():
        for rows, value in each_product(parts_of(merge_refs), row_starts(height, n, 1), hb_ref[...]):
            store(rows, value.astype(jnp.bfloat16))

    @pl.when(jnp.logical_not(left))
    def _():
        store(pl.ds(0, height), hb_ref[...])


def first_sends(spikes, merge_own, levels, cols):
    n = len(spikes)
    size, height = merge_own.shape[1:]
    cut = min(128, height)

    def body(*refs):
        spike_refs, merge_ref = refs[:n], refs[n]
        q_out, first, later = refs[n + 1 :]
        device = lax.axis_index("slab")
        level_left = lowest_bit(device + 1, levels)
        level_right = lowest_bit(device, levels)

        starts = row_starts(height, n, 1)
        for k in range(height // cut):
            window = pl.ds(k * cut, cut)
            value = 0.0
            for spike, start in zip(spike_refs, starts):
                field = jnp.concatenate([spike[p, level_left, :, window] for p in range(2)], axis=1)
                piece = tuple(lambda p=p, start=start: merge_ref[p, :, rows_of(start, size)] for p in range(2))
                for _, part in each_product([piece], [0], field):
                    value += part
            q_out[0, :, window] = value[:, :cut].astype(jnp.bfloat16)
            q_out[1, :, window] = value[:, cut:].astype(jnp.bfloat16)

        share = size // cols
        rows = rows_of(lax.axis_index("col") * share, share) if cols > 1 else pl.ds(0, size)

        @pl.when(is_even())
        def _():
            first[...] = q_out[:, rows, :]
            for p in range(2):
                later[p] = spike_refs[0][p, level_right]

        @pl.when(jnp.logical_not(is_even()))
        def _():
            for p in range(2):
                first[p] = spike_refs[0][p, 0, rows, :]
            later[...] = q_out[...]

    return call(
        body,
        [jax.ShapeDtypeStruct((2, rows, height), jnp.bfloat16) for rows in (size, size // cols, size)],
        [],
        *spikes, merge_own,
        flops=product_flops(height, height),
    )


def first_field(merge, hb):
    height, width = hb.shape
    n = len(merge)

    def body(*refs):
        merge_refs, hb_ref, out = refs[:n], refs[n], refs[n + 1]

        def store(rows, value):
            out[rows, :] = value

        send_field(False, merge_refs, height, hb_ref, store)

    (out,) = call(
        body, [jax.ShapeDtypeStruct(hb.shape, jnp.bfloat16)], [], *merge, hb, flops=product_flops(height, width)
    )
    return out


def merge_tip(left, q_refs, mats, height, mine, got, source, store):
    n = len(q_refs)
    starts = row_starts(height, n, 1)

    @pl.when(left)
    def _():
        for rows, value in each_product(parts_of(q_refs), starts, got[pl.ds(0, height), :]):
            source[rows, :] = (mine[rows, :].astype(jnp.float32) - value).astype(jnp.bfloat16)

    @pl.when(jnp.logical_not(left))
    def _():
        source[...] = mine[pl.ds(0, height), :]

    starts = row_starts(height, n, len(mats) // n)
    for rows, value in each_product(mats, starts, source[...]):
        store(rows, (got[rows, :].astype(jnp.float32) - value).astype(jnp.bfloat16))


def first_level(state, mine, got, mats, q, spikes, merge):
    height, width = state.shape
    n = len(q)

    def body(*refs):
        state_ref, mine_ref, got_ref = refs[:3]
        mat_refs, rest = refs[3 : 3 + len(mats)], refs[3 + len(mats) :]
        q_refs, spike_refs, merge_refs = (rest[k * n : (k + 1) * n] for k in range(3))
        out, send, source, tip = rest[3 * n :]

        def store_tip(rows, value):
            tip[rows, :] = value

        merge_tip(is_even(), q_refs, parts_of(mat_refs), height, mine_ref, got_ref, source, store_tip)
        for rows, value in each_product(at_level(spike_refs, 0), row_starts(height, n, 1), tip[...]):
            new = state_ref[rows, :] - value
            out[rows, :] = new
            source[rows, :] = new.astype(jnp.bfloat16)

        def store(rows, value):
            send[rows, :] = value

        send_field(True, merge_refs, height, source, store)

    return call(
        body,
        [jax.ShapeDtypeStruct((height, width), t) for t in (jnp.float32, jnp.bfloat16)],
        [pltpu.VMEM((height, width), jnp.bfloat16)] * 2,
        state, mine, got, *mats, *q, *spikes, *merge,
        flops=4 * product_flops(height, width),
    )


def later_tip(position, span, mine, got, mats, q):
    height, width = mine.shape
    n = len(q)

    def body(*refs):
        mine_ref, got_ref = refs[:2]
        mat_refs, q_refs = refs[2 : 2 + n], refs[2 + n : 2 + 2 * n]
        out, source = refs[2 + 2 * n :]
        place = position()

        def store(rows, value):
            out[rows, :] = value

        @pl.when(jnp.logical_or(place == span - 1, place == span))
        def _():
            merge_tip(place == span - 1, q_refs, parts_of(mat_refs), height, mine_ref, got_ref, source, store)

    (tip,) = call(
        body,
        [jax.ShapeDtypeStruct((height, width), jnp.bfloat16)],
        [pltpu.VMEM((height, width), jnp.bfloat16)],
        mine, got, *mats, *q,
        flops=2 * product_flops(height, width),
    )
    return tip


def pick(use_new, new, old):
    def body(new_ref, old_ref, out):
        @pl.when(use_new())
        def _():
            out[...] = new_ref[...]

        @pl.when(jnp.logical_not(use_new()))
        def _():
            out[...] = old_ref[...]

    (out,) = call(body, [jax.ShapeDtypeStruct(old.shape, old.dtype)], [], new, old)
    return out


def tip_update(use_new, state, new_tip, tip, spikes, level, merge=()):
    height, width = state.shape
    n = len(spikes)
    kinds = (jnp.float32, jnp.bfloat16) if merge else (jnp.float32,)

    def body(*refs):
        state_ref, new_ref, tip_ref = refs[:3]
        spike_refs, merge_refs = refs[3 : 3 + n], refs[3 + n : 3 + n + len(merge)]
        outs, source = refs[3 + n + len(merge) : -1], refs[-1]

        @pl.when(use_new())
        def _():
            source[...] = new_ref[...]

        @pl.when(jnp.logical_not(use_new()))
        def _():
            source[...] = tip_ref[...]

        starts = row_starts(height, n, 1)
        for rows, value in each_product(at_level(spike_refs, level), starts, source[...]):
            outs[0][rows, :] = state_ref[rows, :] - value
        if not merge:
            return
        source[...] = outs[0][...].astype(jnp.bfloat16)

        def store(rows, value):
            outs[1][rows, :] = value

        send_field(True, merge_refs, height, source, store)

    return call(
        body,
        [jax.ShapeDtypeStruct((height, width), t) for t in kinds],
        [pltpu.VMEM((height, width), jnp.bfloat16)],
        state, new_tip, tip, *spikes, *merge,
        flops=product_flops(height, width),
    )


def last_update(use_new, done, state, new_tip, tip, spikes, level):
    height, width = state.shape
    n, k = len(spikes), len(done)
    own = width // 2
    before = sum(d.shape[1] // 2 for d in done)
    columns = before + own
    split = before - before % 128

    def body(*refs):
        done_refs = refs[:k]
        state_ref, new_ref, tip_ref = refs[k : k + 3]
        spike_refs = refs[k + 3 : k + 3 + n]
        out, source, whole, sems = refs[k + 3 + n :]

        first = 0
        for d in done_refs:
            w = d.shape[1] // 2
            whole[0, :, pl.ds(first, w)] = d[:, :w]
            whole[1, :, pl.ds(first, w)] = d[:, w:]
            first += w
        copies = []
        if split:
            window = pl.ds(0, split)
            copies.append(pltpu.make_async_copy(whole.at[:, :, window], out.at[:, :, window], sems.at[0]))
            copies[0].start()

        @pl.when(use_new())
        def _():
            source[...] = new_ref[...]

        @pl.when(jnp.logical_not(use_new()))
        def _():
            source[...] = tip_ref[...]

        starts = row_starts(height, n, 1)
        for rows, value in each_product(at_level(spike_refs, level), starts, source[...]):
            new = state_ref[rows, :] - value
            whole[0, rows, pl.ds(before, own)] = new[:, :own]
            whole[1, rows, pl.ds(before, own)] = new[:, own:]
        window = pl.ds(split, columns - split)
        copies.append(pltpu.make_async_copy(whole.at[:, :, window], out.at[:, :, window], sems.at[1]))
        copies[-1].start()
        for copy in copies:
            copy.wait()

    return pl.pallas_call(
        body,
        out_shape=jax.ShapeDtypeStruct((2, height, columns), jnp.float32),
        in_specs=[VMEM] * (k + 3 + n),
        out_specs=pl.BlockSpec(memory_space=pl.ANY),
        scratch_shapes=[
            pltpu.VMEM((height, width), jnp.bfloat16),
            pltpu.VMEM((2, height, columns), jnp.float32),
            pltpu.SemaphoreType.DMA((2,)),
        ],
        compiler_params=pltpu.CompilerParams(vmem_limit_bytes=24 * 2**20),
        cost_estimate=pl.CostEstimate(
            flops=product_flops(height, width), bytes_accessed=12 * height * columns, transcendentals=0
        ),
    )(*done, state, new_tip, tip, *spikes)


def swap(block, pairs):
    return lax.ppermute(block, "slab", pairs + [(b, a) for a, b in pairs])


def per_device(widths, rhs, dinv, spikes, merge_inv):
    slabs = lax.axis_size("slab")
    levels = spikes.shape[2]
    chunks = range(len(widths))

    cols = lax.axis_size("col")
    spike_all = ring_gather(spikes[:, 0], "orb")
    spike_own, merge_own = fetch(spikes[:, 0], merge_inv[:, 0])
    spike_all[0] = spike_own
    q_own, first, later = first_sends(spike_all, merge_own, levels, cols)
    pairs = [(i, i + 1) for i in range(0, slabs, 2)]
    first = swap(first, pairs)
    later = swap(later, [(i, i + 1) for i in range(1, slabs - 1, 2)])
    q = ring_gather(q_own, "orb")
    dinv, merge_inv, _ = lax.optimization_barrier((dinv, merge_inv, q_own))
    inverse = ring_gather(dinv[:, 0], "orb")
    merge = [merge_own] + ring_gather(merge_inv[:, 0], "orb")[1:]
    states, sends, gots = [], [], []
    for c in chunks:
        state, hb = start_state(inverse, rhs[:, 0], sum(widths[:c]), widths[c])
        states.append(state)
        sends.append(first_field(merge, hb))
        gots.append(swap(sends[c], pairs))
    first, _ = lax.optimization_barrier((first, sends[-1]))
    across = [ring_gather(p, "orb") for p in ring_gather(first, "col")]
    first = [across[k][j] for j in range(len(q)) for k in range(cols)]
    later = ring_gather(later, "orb")
    for c in chunks:
        states[c], sends[c] = first_level(states[c], sends[c], gots[c], first, q, spike_all, merge)

    for level in range(1, levels):
        span = 1 << level
        heads = range(0, slabs, 2 * span)

        def position(span=span):
            return lax.rem(lax.axis_index("slab"), 2 * span)

        gots = [swap(sends[c], [(g + span - 1, g + span) for g in heads]) for c in chunks]
        tips = [later_tip(position, span, sends[c], gots[c], later, q) for c in chunks]
        reach = 1
        while reach < span:
            route = []
            for g in heads:
                for j in range(reach):
                    if j + reach < span:
                        route.append((g + span + j, g + span + j + reach))
                        route.append((g + span - 1 - j, g + span - 1 - j - reach))
            moved = [lax.ppermute(tips[c], "slab", route) for c in chunks]

            def is_new(span=span, position=position, reach=reach):
                far = jnp.where(position() >= span, position() - span, span - 1 - position())
                return jnp.logical_and(far >= reach, far < 2 * reach)

            if 2 * reach < span:
                tips = [pick(is_new, moved[c], tips[c]) for c in chunks]
            reach *= 2
        if level < levels - 1:
            for c in chunks:
                states[c], sends[c] = tip_update(is_new, states[c], moved[c], tips[c], spike_all, level, merge)
            continue
        for c in chunks[:-1]:
            (states[c],) = tip_update(is_new, states[c], moved[c], tips[c], spike_all, level)
        c = chunks[-1]
        whole = last_update(is_new, states[:c], states[c], moved[c], tips[c], spike_all, level)
    return whole[:, None]


def chunk_widths(columns):
    total = sum(SHARES)
    if columns * min(SHARES) // total < 64:
        return [columns]
    return [columns * s // total for s in SHARES]


def solution(mesh):
    placed = (
        P(None, ("energy", "slab"), None, ("col", "orb")),
        P(None, ("energy", "slab"), "orb", None),
        P(None, ("energy", "slab"), None, "orb", None),
        P(None, ("energy", "slab"), "orb", None),
    )

    def body(rhs, dinv, spikes, merge_inv):
        return per_device(chunk_widths(rhs.shape[3]), rhs, dinv, spikes, merge_inv)

    return jax.shard_map(
        body,
        mesh=mesh,
        in_specs=placed,
        out_specs=P(None, ("energy", "slab"), None, ("col", "orb")),
        check_vma=False,
    )
```

```python
import jax
import jax.numpy as jnp
from jax import lax
from jax.experimental import pallas as pl
from jax.experimental.pallas import tpu as pltpu
from jax.sharding import PartitionSpec as P

VMEM = pl.BlockSpec(memory_space=pltpu.VMEM)
SHARES = (1, 1)


def ring_gather(block, axis):
    count = lax.axis_size(axis)
    blocks = [block]
    for step in range(1, count):
        blocks.append(lax.ppermute(block, axis, [((i + step) % count, i) for i in range(count)]))
    return blocks


def row_starts(height, orb_count, col_parts):
    orb = lax.axis_index("orb")
    per_orb = height // orb_count
    starts = []
    for j in range(orb_count):
        base = lax.rem(orb + j, orb_count) * per_orb
        if col_parts == 1:
            starts.append(base)
            continue
        col = lax.axis_index("col")
        for k in range(col_parts):
            starts.append(base + lax.rem(col + k, col_parts) * (per_orb // col_parts))
    return starts


def rows_of(start, size):
    return pl.ds(pl.multiple_of(start, size), size)


def turned(field):
    half = field.shape[1] // 2
    return jnp.concatenate([-field[:, half:], field[:, :half]], axis=1)


def at_level(spikes, level):
    return [tuple(lambda s=s, p=p: s[p, level] for p in range(2)) for s in spikes]


def parts_of(pieces):
    return [tuple(lambda m=m, p=p: m[p] for p in range(2)) for m in pieces]


def each_product(pieces, starts, field):
    field_i = turned(field)
    for (real, imag), start in zip(pieces, starts):
        value = jnp.dot(real(), field, preferred_element_type=jnp.float32)
        value += jnp.dot(imag(), field_i, preferred_element_type=jnp.float32)
        yield rows_of(start, value.shape[0]), value


def call(body, outs, scratch, *args, flops=0, aliases=None):
    nbytes = sum(a.size * a.dtype.itemsize for a in args) + sum(o.size * o.dtype.itemsize for o in outs)
    return pl.pallas_call(
        body,
        out_shape=outs,
        in_specs=[VMEM] * len(args),
        out_specs=[VMEM] * len(outs),
        scratch_shapes=scratch,
        compiler_params=pltpu.CompilerParams(vmem_limit_bytes=24 * 2**20),
        cost_estimate=pl.CostEstimate(flops=flops, bytes_accessed=nbytes, transcendentals=0),
    )(*args)


def product_flops(height, width):
    return 2 * 2 * height * height * width


def is_even():
    return lax.rem(lax.axis_index("slab"), 2) == 0


def lowest_bit(number, levels):
    found = jnp.int32(0)
    for level in range(1, levels):
        found = jnp.where(lax.rem(number, 1 << level) == 0, level, found)
    return found


def fetch(*arrays):
    n = len(arrays)

    def body(*refs):
        sems = refs[-1]
        copies = [pltpu.make_async_copy(refs[k], refs[n + k], sems.at[k]) for k in range(n)]
        for copy in copies:
            copy.start()
        for copy in copies:
            copy.wait()

    return pl.pallas_call(
        body,
        out_shape=[jax.ShapeDtypeStruct(a.shape, a.dtype) for a in arrays],
        in_specs=[pl.BlockSpec(memory_space=pl.ANY)] * n,
        out_specs=[VMEM] * n,
        scratch_shapes=[pltpu.SemaphoreType.DMA((n,))],
        compiler_params=pltpu.CompilerParams(vmem_limit_bytes=48 * 2**20),
        cost_estimate=pl.CostEstimate(flops=0, bytes_accessed=2 * sum(a.size * 2 for a in arrays), transcendentals=0),
    )(*arrays)


def start_state(pieces, rhs, first, width):
    height = rhs.shape[1]
    n = len(pieces)

    def body(*refs):
        mats, rhs_ref, (out, out_b) = refs[:n], refs[n], refs[n + 1 :]
        window = pl.ds(first, width)
        field = jnp.concatenate([rhs_ref[0, :, window], rhs_ref[1, :, window]], axis=1)
        for rows, value in each_product(parts_of(mats), row_starts(height, n, 1), field):
            out[rows, :] = value
            out_b[rows, :] = value.astype(jnp.bfloat16)

    outs = [jax.ShapeDtypeStruct((height, 2 * width), t) for t in (jnp.float32, jnp.bfloat16)]
    return call(body, outs, [], *pieces, rhs, flops=product_flops(height, 2 * width))


def send_field(odd_sends_product, merge_refs, height, hb_ref, store):
    n = len(merge_refs)
    left = jnp.logical_xor(is_even(), odd_sends_product)

    @pl.when(left)
    def _():
        for rows, value in each_product(parts_of(merge_refs), row_starts(height, n, 1), hb_ref[...]):
            store(rows, value.astype(jnp.bfloat16))

    @pl.when(jnp.logical_not(left))
    def _():
        store(pl.ds(0, height), hb_ref[...])


def first_sends(spikes, merge_own, levels, cols):
    n = len(spikes)
    size, height = merge_own.shape[1:]
    cut = min(128, height)

    def body(*refs):
        spike_refs, merge_ref = refs[:n], refs[n]
        q_out, first, later = refs[n + 1 :]
        device = lax.axis_index("slab")
        level_left = lowest_bit(device + 1, levels)
        level_right = lowest_bit(device, levels)

        starts = row_starts(height, n, 1)
        for k in range(height // cut):
            window = pl.ds(k * cut, cut)
            value = 0.0
            for spike, start in zip(spike_refs, starts):
                field = jnp.concatenate([spike[p, level_left, :, window] for p in range(2)], axis=1)
                piece = tuple(lambda p=p, start=start: merge_ref[p, :, rows_of(start, size)] for p in range(2))
                for _, part in each_product([piece], [0], field):
                    value += part
            q_out[0, :, window] = value[:, :cut].astype(jnp.bfloat16)
            q_out[1, :, window] = value[:, cut:].astype(jnp.bfloat16)

        share = size // cols
        rows = rows_of(lax.axis_index("col") * share, share) if cols > 1 else pl.ds(0, size)

        @pl.when(is_even())
        def _():
            first[...] = q_out[:, rows, :]
            for p in range(2):
                later[p] = spike_refs[0][p, level_right]

        @pl.when(jnp.logical_not(is_even()))
        def _():
            for p in range(2):
                first[p] = spike_refs[0][p, 0, rows, :]
            later[...] = q_out[...]

    return call(
        body,
        [jax.ShapeDtypeStruct((2, rows, height), jnp.bfloat16) for rows in (size, size // cols, size)],
        [],
        *spikes, merge_own,
        flops=product_flops(height, height),
    )


def first_field(merge, hb):
    height, width = hb.shape
    n = len(merge)

    def body(*refs):
        merge_refs, hb_ref, out = refs[:n], refs[n], refs[n + 1]

        def store(rows, value):
            out[rows, :] = value

        send_field(False, merge_refs, height, hb_ref, store)

    (out,) = call(
        body, [jax.ShapeDtypeStruct(hb.shape, jnp.bfloat16)], [], *merge, hb, flops=product_flops(height, width)
    )
    return out


def source_of(left, q_refs, height, mine, got, source):
    @pl.when(left)
    def _():
        starts = row_starts(height, len(q_refs), 1)
        for rows, value in each_product(parts_of(q_refs), starts, got[pl.ds(0, height), :]):
            source[rows, :] = (mine[rows, :].astype(jnp.float32) - value).astype(jnp.bfloat16)

    @pl.when(jnp.logical_not(left))
    def _():
        source[...] = mine[pl.ds(0, height), :]


def tip_from(mats, orb_count, height, source, got, store):
    starts = row_starts(height, orb_count, len(mats) // orb_count)
    for rows, value in each_product(mats, starts, source[...]):
        store(rows, (got[rows, :].astype(jnp.float32) - value).astype(jnp.bfloat16))


def first_source(mine, got, q):
    height, width = mine.shape
    n = len(q)

    def body(*refs):
        mine_ref, got_ref = refs[:2]
        source_of(is_even(), refs[2 : 2 + n], height, mine_ref, got_ref, refs[2 + n])

    (source,) = call(
        body,
        [jax.ShapeDtypeStruct((height, width), jnp.bfloat16)],
        [],
        mine, got, *q,
        flops=product_flops(height, width),
    )
    return source


def merge_tip(left, q_refs, mats, height, mine, got, source, store):
    source_of(left, q_refs, height, mine, got, source)
    tip_from(mats, len(q_refs), height, source, got, store)


def first_level(state, source, got, mats, spikes, merge):
    height, width = state.shape
    n = len(spikes)

    def body(*refs):
        state_ref, source_ref, got_ref = refs[:3]
        mat_refs, rest = refs[3 : 3 + len(mats)], refs[3 + len(mats) :]
        spike_refs, merge_refs = rest[:n], rest[n : 2 * n]
        out, send, rounded, tip = rest[2 * n :]

        def store_tip(rows, value):
            tip[rows, :] = value

        tip_from(parts_of(mat_refs), n, height, source_ref, got_ref, store_tip)
        for rows, value in each_product(at_level(spike_refs, 0), row_starts(height, n, 1), tip[...]):
            new = state_ref[rows, :] - value
            out[rows, :] = new
            rounded[rows, :] = new.astype(jnp.bfloat16)

        def store(rows, value):
            send[rows, :] = value

        send_field(True, merge_refs, height, rounded, store)

    return call(
        body,
        [jax.ShapeDtypeStruct((height, width), t) for t in (jnp.float32, jnp.bfloat16)],
        [pltpu.VMEM((height, width), jnp.bfloat16)] * 2,
        state, source, got, *mats, *spikes, *merge,
        flops=3 * product_flops(height, width),
    )


def later_tip(position, span, mine, got, mats, q):
    height, width = mine.shape
    n = len(q)

    def body(*refs):
        mine_ref, got_ref = refs[:2]
        mat_refs, q_refs = refs[2 : 2 + n], refs[2 + n : 2 + 2 * n]
        out, source = refs[2 + 2 * n :]
        place = position()

        def store(rows, value):
            out[rows, :] = value

        @pl.when(jnp.logical_or(place == span - 1, place == span))
        def _():
            merge_tip(place == span - 1, q_refs, parts_of(mat_refs), height, mine_ref, got_ref, source, store)

    (tip,) = call(
        body,
        [jax.ShapeDtypeStruct((height, width), jnp.bfloat16)],
        [pltpu.VMEM((height, width), jnp.bfloat16)],
        mine, got, *mats, *q,
        flops=2 * product_flops(height, width),
    )
    return tip


def pick(use_new, new, old):
    def body(new_ref, old_ref, out):
        @pl.when(use_new())
        def _():
            out[...] = new_ref[...]

        @pl.when(jnp.logical_not(use_new()))
        def _():
            out[...] = old_ref[...]

    (out,) = call(body, [jax.ShapeDtypeStruct(old.shape, old.dtype)], [], new, old)
    return out


def tip_update(use_new, state, new_tip, tip, spikes, level, merge=()):
    height, width = state.shape
    n = len(spikes)
    kinds = (jnp.float32, jnp.bfloat16) if merge else (jnp.float32,)

    def body(*refs):
        state_ref, new_ref, tip_ref = refs[:3]
        spike_refs, merge_refs = refs[3 : 3 + n], refs[3 + n : 3 + n + len(merge)]
        outs, source = refs[3 + n + len(merge) : -1], refs[-1]

        @pl.when(use_new())
        def _():
            source[...] = new_ref[...]

        @pl.when(jnp.logical_not(use_new()))
        def _():
            source[...] = tip_ref[...]

        starts = row_starts(height, n, 1)
        for rows, value in each_product(at_level(spike_refs, level), starts, source[...]):
            outs[0][rows, :] = state_ref[rows, :] - value
        if not merge:
            return
        source[...] = outs[0][...].astype(jnp.bfloat16)

        def store(rows, value):
            outs[1][rows, :] = value

        send_field(True, merge_refs, height, source, store)

    return call(
        body,
        [jax.ShapeDtypeStruct((height, width), t) for t in kinds],
        [pltpu.VMEM((height, width), jnp.bfloat16)],
        state, new_tip, tip, *spikes, *merge,
        flops=product_flops(height, width),
    )


def last_update(use_new, done, state, new_tip, tip, spikes, level):
    height, width = state.shape
    n, k = len(spikes), len(done)
    own = width // 2
    before = sum(d.shape[1] // 2 for d in done)
    columns = before + own
    split = before - before % 128

    def body(*refs):
        done_refs = refs[:k]
        state_ref, new_ref, tip_ref = refs[k : k + 3]
        spike_refs = refs[k + 3 : k + 3 + n]
        out, source, whole, sems = refs[k + 3 + n :]

        first = 0
        for d in done_refs:
            w = d.shape[1] // 2
            whole[0, :, pl.ds(first, w)] = d[:, :w]
            whole[1, :, pl.ds(first, w)] = d[:, w:]
            first += w
        copies = []
        if split:
            window = pl.ds(0, split)
            copies.append(pltpu.make_async_copy(whole.at[:, :, window], out.at[:, :, window], sems.at[0]))
            copies[0].start()

        @pl.when(use_new())
        def _():
            source[...] = new_ref[...]

        @pl.when(jnp.logical_not(use_new()))
        def _():
            source[...] = tip_ref[...]

        starts = row_starts(height, n, 1)
        for rows, value in each_product(at_level(spike_refs, level), starts, source[...]):
            new = state_ref[rows, :] - value
            whole[0, rows, pl.ds(before, own)] = new[:, :own]
            whole[1, rows, pl.ds(before, own)] = new[:, own:]
        window = pl.ds(split, columns - split)
        copies.append(pltpu.make_async_copy(whole.at[:, :, window], out.at[:, :, window], sems.at[1]))
        copies[-1].start()
        for copy in copies:
            copy.wait()

    return pl.pallas_call(
        body,
        out_shape=jax.ShapeDtypeStruct((2, height, columns), jnp.float32),
        in_specs=[VMEM] * (k + 3 + n),
        out_specs=pl.BlockSpec(memory_space=pl.ANY),
        scratch_shapes=[
            pltpu.VMEM((height, width), jnp.bfloat16),
            pltpu.VMEM((2, height, columns), jnp.float32),
            pltpu.SemaphoreType.DMA((2,)),
        ],
        compiler_params=pltpu.CompilerParams(vmem_limit_bytes=24 * 2**20),
        cost_estimate=pl.CostEstimate(
            flops=product_flops(height, width), bytes_accessed=12 * height * columns, transcendentals=0
        ),
    )(*done, state, new_tip, tip, *spikes)


def swap(block, pairs):
    return lax.ppermute(block, "slab", pairs + [(b, a) for a, b in pairs])


def per_device(widths, rhs, dinv, spikes, merge_inv):
    slabs = lax.axis_size("slab")
    levels = spikes.shape[2]
    chunks = range(len(widths))

    cols = lax.axis_size("col")
    spike_all = ring_gather(spikes[:, 0], "orb")
    spike_own, merge_own = fetch(spikes[:, 0], merge_inv[:, 0])
    spike_all[0] = spike_own
    q_own, first, later = first_sends(spike_all, merge_own, levels, cols)
    pairs = [(i, i + 1) for i in range(0, slabs, 2)]
    first = swap(first, pairs)
    later = swap(later, [(i, i + 1) for i in range(1, slabs - 1, 2)])
    q = ring_gather(q_own, "orb")
    dinv, merge_inv, _ = lax.optimization_barrier((dinv, merge_inv, q_own))
    inverse = ring_gather(dinv[:, 0], "orb")
    merge = [merge_own] + ring_gather(merge_inv[:, 0], "orb")[1:]
    states, sends, gots = [], [], []
    for c in chunks:
        state, hb = start_state(inverse, rhs[:, 0], sum(widths[:c]), widths[c])
        states.append(state)
        sends.append(first_field(merge, hb))
        gots.append(swap(sends[c], pairs))
    first, _ = lax.optimization_barrier((first, sends[-1]))
    sources = [first_source(sends[0], gots[0], q)]
    *across, _ = lax.optimization_barrier((*ring_gather(first, "col"), sources[0]))
    across = [ring_gather(p, "orb") for p in across]
    first = [across[k][j] for j in range(len(q)) for k in range(cols)]
    later = ring_gather(later, "orb")
    for c in chunks:
        if c:
            mine, _ = lax.optimization_barrier((sends[c], across[-1][-1]))
            sources.append(first_source(mine, gots[c], q))
        states[c], sends[c] = first_level(states[c], sources[c], gots[c], first, spike_all, merge)

    for level in range(1, levels):
        span = 1 << level
        heads = range(0, slabs, 2 * span)

        def position(span=span):
            return lax.rem(lax.axis_index("slab"), 2 * span)

        gots = [swap(sends[c], [(g + span - 1, g + span) for g in heads]) for c in chunks]
        tips = [later_tip(position, span, sends[c], gots[c], later, q) for c in chunks]
        reach = 1
        while reach < span:
            route = []
            for g in heads:
                for j in range(reach):
                    if j + reach < span:
                        route.append((g + span + j, g + span + j + reach))
                        route.append((g + span - 1 - j, g + span - 1 - j - reach))
            moved = [lax.ppermute(tips[c], "slab", route) for c in chunks]

            def is_new(span=span, position=position, reach=reach):
                far = jnp.where(position() >= span, position() - span, span - 1 - position())
                return jnp.logical_and(far >= reach, far < 2 * reach)

            if 2 * reach < span:
                tips = [pick(is_new, moved[c], tips[c]) for c in chunks]
            reach *= 2
        if level < levels - 1:
            for c in chunks:
                states[c], sends[c] = tip_update(is_new, states[c], moved[c], tips[c], spike_all, level, merge)
            continue
        for c in chunks[:-1]:
            (states[c],) = tip_update(is_new, states[c], moved[c], tips[c], spike_all, level)
        c = chunks[-1]
        whole = last_update(is_new, states[:c], states[c], moved[c], tips[c], spike_all, level)
    return whole[:, None]


def chunk_widths(columns):
    total = sum(SHARES)
    if columns * min(SHARES) // total < 64:
        return [columns]
    return [columns * s // total for s in SHARES]


def solution(mesh):
    placed = (
        P(None, ("energy", "slab"), None, ("col", "orb")),
        P(None, ("energy", "slab"), "orb", None),
        P(None, ("energy", "slab"), None, "orb", None),
        P(None, ("energy", "slab"), "orb", None),
    )

    def body(rhs, dinv, spikes, merge_inv):
        return per_device(chunk_widths(rhs.shape[3]), rhs, dinv, spikes, merge_inv)

    return jax.shard_map(
        body,
        mesh=mesh,
        in_specs=placed,
        out_specs=P(None, ("energy", "slab"), None, ("col", "orb")),
        check_vma=False,
    )
```

```python
import jax
import jax.numpy as jnp
from jax import lax
from jax.experimental import pallas as pl
from jax.experimental.pallas import tpu as pltpu
from jax.sharding import PartitionSpec as P

VMEM = pl.BlockSpec(memory_space=pltpu.VMEM)
SHARES = (1, 1)


def ring_gather(block, axis):
    count = lax.axis_size(axis)
    blocks = [block]
    for step in range(1, count):
        blocks.append(lax.ppermute(block, axis, [((i + step) % count, i) for i in range(count)]))
    return blocks


def row_starts(height, orb_count, col_parts):
    orb = lax.axis_index("orb")
    per_orb = height // orb_count
    starts = []
    for j in range(orb_count):
        base = lax.rem(orb + j, orb_count) * per_orb
        if col_parts == 1:
            starts.append(base)
            continue
        col = lax.axis_index("col")
        for k in range(col_parts):
            starts.append(base + lax.rem(col + k, col_parts) * (per_orb // col_parts))
    return starts


def rows_of(start, size):
    return pl.ds(pl.multiple_of(start, size), size)


def turned(field):
    half = field.shape[1] // 2
    return jnp.concatenate([-field[:, half:], field[:, :half]], axis=1)


def at_level(spikes, level):
    return [tuple(lambda s=s, p=p: s[p, level] for p in range(2)) for s in spikes]


def parts_of(pieces):
    return [tuple(lambda m=m, p=p: m[p] for p in range(2)) for m in pieces]


def each_product(pieces, starts, field):
    field_i = turned(field)
    for (real, imag), start in zip(pieces, starts):
        value = jnp.dot(real(), field, preferred_element_type=jnp.float32)
        value += jnp.dot(imag(), field_i, preferred_element_type=jnp.float32)
        yield rows_of(start, value.shape[0]), value


def call(body, outs, scratch, *args, flops=0, aliases=None):
    nbytes = sum(a.size * a.dtype.itemsize for a in args) + sum(o.size * o.dtype.itemsize for o in outs)
    return pl.pallas_call(
        body,
        out_shape=outs,
        in_specs=[VMEM] * len(args),
        out_specs=[VMEM] * len(outs),
        scratch_shapes=scratch,
        compiler_params=pltpu.CompilerParams(vmem_limit_bytes=24 * 2**20),
        cost_estimate=pl.CostEstimate(flops=flops, bytes_accessed=nbytes, transcendentals=0),
    )(*args)


def product_flops(height, width):
    return 2 * 2 * height * height * width


def is_even():
    return lax.rem(lax.axis_index("slab"), 2) == 0


def lowest_bit(number, levels):
    found = jnp.int32(0)
    for level in range(1, levels):
        found = jnp.where(lax.rem(number, 1 << level) == 0, level, found)
    return found


def fetch(*arrays):
    n = len(arrays)

    def body(*refs):
        sems = refs[-1]
        copies = [pltpu.make_async_copy(refs[k], refs[n + k], sems.at[k]) for k in range(n)]
        for copy in copies:
            copy.start()
        for copy in copies:
            copy.wait()

    return pl.pallas_call(
        body,
        out_shape=[jax.ShapeDtypeStruct(a.shape, a.dtype) for a in arrays],
        in_specs=[pl.BlockSpec(memory_space=pl.ANY)] * n,
        out_specs=[VMEM] * n,
        scratch_shapes=[pltpu.SemaphoreType.DMA((n,))],
        compiler_params=pltpu.CompilerParams(vmem_limit_bytes=48 * 2**20),
        cost_estimate=pl.CostEstimate(flops=0, bytes_accessed=2 * sum(a.size * 2 for a in arrays), transcendentals=0),
    )(*arrays)


def start_state(pieces, rhs, first, width):
    height = rhs.shape[1]
    n = len(pieces)

    def body(*refs):
        mats, rhs_ref, (out, out_b) = refs[:n], refs[n], refs[n + 1 :]
        window = pl.ds(first, width)
        field = jnp.concatenate([rhs_ref[0, :, window], rhs_ref[1, :, window]], axis=1)
        for rows, value in each_product(parts_of(mats), row_starts(height, n, 1), field):
            out[rows, :] = value
            out_b[rows, :] = value.astype(jnp.bfloat16)

    outs = [jax.ShapeDtypeStruct((height, 2 * width), t) for t in (jnp.float32, jnp.bfloat16)]
    return call(body, outs, [], *pieces, rhs, flops=product_flops(height, 2 * width))


def send_field(odd_sends_product, merge_refs, height, hb_ref, store):
    n = len(merge_refs)
    left = jnp.logical_xor(is_even(), odd_sends_product)

    @pl.when(left)
    def _():
        for rows, value in each_product(parts_of(merge_refs), row_starts(height, n, 1), hb_ref[...]):
            store(rows, value.astype(jnp.bfloat16))

    @pl.when(jnp.logical_not(left))
    def _():
        store(pl.ds(0, height), hb_ref[...])


def first_matrix(spikes, merge_own, levels, cols):
    n = len(spikes)
    size, height = merge_own.shape[1:]
    share = size // cols
    cut = min(128, height)

    def body(*refs):
        spike_refs, merge_ref, out = refs[:n], refs[n], refs[n + 1]
        rows = rows_of(lax.axis_index("col") * share, share)

        @pl.when(is_even())
        def _():
            own_product(spike_refs, merge_ref, rows, 0, cut, out)

        @pl.when(jnp.logical_not(is_even()))
        def _():
            for p in range(2):
                out[p] = spike_refs[0][p, 0, rows, :]

    (out,) = call(
        body,
        [jax.ShapeDtypeStruct((2, share, height), jnp.bfloat16)],
        [],
        *spikes, merge_own,
        flops=product_flops(height, height) // cols,
    )
    return out


def own_product(spike_refs, merge_ref, rows, level, cut, out):
    n = len(spike_refs)
    height = out.shape[2]
    size = height // n
    starts = row_starts(height, n, 1)
    for k in range(height // cut):
        window = pl.ds(k * cut, cut)
        value = 0.0
        for spike, start in zip(spike_refs, starts):
            field = jnp.concatenate([spike[p, level, :, window] for p in range(2)], axis=1)
            piece = tuple(lambda p=p, start=start: merge_ref[p, rows, rows_of(start, size)] for p in range(2))
            for _, part in each_product([piece], [0], field):
                value += part
        out[0, :, window] = value[:, :cut].astype(jnp.bfloat16)
        out[1, :, window] = value[:, cut:].astype(jnp.bfloat16)


def own_matrix(spikes, merge_own, levels):
    n = len(spikes)
    size, height = merge_own.shape[1:]
    cut = min(128, height)

    def body(*refs):
        spike_refs, merge_ref = refs[:n], refs[n]
        q_out, later = refs[n + 1 :]
        device = lax.axis_index("slab")
        own_product(spike_refs, merge_ref, pl.ds(0, size), lowest_bit(device + 1, levels), cut, q_out)
        level_right = lowest_bit(device, levels)

        @pl.when(is_even())
        def _():
            for p in range(2):
                later[p] = spike_refs[0][p, level_right]

        @pl.when(jnp.logical_not(is_even()))
        def _():
            later[...] = q_out[...]

    return call(
        body,
        [jax.ShapeDtypeStruct((2, size, height), jnp.bfloat16)] * 2,
        [],
        *spikes, merge_own,
        flops=product_flops(height, height),
    )


def first_field(merge, hb):
    height, width = hb.shape
    n = len(merge)

    def body(*refs):
        merge_refs, hb_ref, out = refs[:n], refs[n], refs[n + 1]

        def store(rows, value):
            out[rows, :] = value

        send_field(False, merge_refs, height, hb_ref, store)

    (out,) = call(
        body, [jax.ShapeDtypeStruct(hb.shape, jnp.bfloat16)], [], *merge, hb, flops=product_flops(height, width)
    )
    return out


def source_of(left, q_refs, height, mine, got, source):
    @pl.when(left)
    def _():
        starts = row_starts(height, len(q_refs), 1)
        for rows, value in each_product(parts_of(q_refs), starts, got[pl.ds(0, height), :]):
            source[rows, :] = (mine[rows, :].astype(jnp.float32) - value).astype(jnp.bfloat16)

    @pl.when(jnp.logical_not(left))
    def _():
        source[...] = mine[pl.ds(0, height), :]


def tip_from(mats, orb_count, height, source, got, store):
    starts = row_starts(height, orb_count, len(mats) // orb_count)
    for rows, value in each_product(mats, starts, source[...]):
        store(rows, (got[rows, :].astype(jnp.float32) - value).astype(jnp.bfloat16))


def first_source(mine, got, q):
    height, width = mine.shape
    n = len(q)

    def body(*refs):
        mine_ref, got_ref = refs[:2]
        source_of(is_even(), refs[2 : 2 + n], height, mine_ref, got_ref, refs[2 + n])

    (source,) = call(
        body,
        [jax.ShapeDtypeStruct((height, width), jnp.bfloat16)],
        [],
        mine, got, *q,
        flops=product_flops(height, width),
    )
    return source


def merge_tip(left, q_refs, mats, height, mine, got, source, store):
    source_of(left, q_refs, height, mine, got, source)
    tip_from(mats, len(q_refs), height, source, got, store)


def first_level(state, source, got, mats, spikes, merge):
    height, width = state.shape
    n = len(spikes)

    def body(*refs):
        state_ref, source_ref, got_ref = refs[:3]
        mat_refs, rest = refs[3 : 3 + len(mats)], refs[3 + len(mats) :]
        spike_refs, merge_refs = rest[:n], rest[n : 2 * n]
        out, send, rounded, tip = rest[2 * n :]

        def store_tip(rows, value):
            tip[rows, :] = value

        tip_from(parts_of(mat_refs), n, height, source_ref, got_ref, store_tip)
        for rows, value in each_product(at_level(spike_refs, 0), row_starts(height, n, 1), tip[...]):
            new = state_ref[rows, :] - value
            out[rows, :] = new
            rounded[rows, :] = new.astype(jnp.bfloat16)

        def store(rows, value):
            send[rows, :] = value

        send_field(True, merge_refs, height, rounded, store)

    return call(
        body,
        [jax.ShapeDtypeStruct((height, width), t) for t in (jnp.float32, jnp.bfloat16)],
        [pltpu.VMEM((height, width), jnp.bfloat16)] * 2,
        state, source, got, *mats, *spikes, *merge,
        flops=3 * product_flops(height, width),
    )


def later_tip(position, span, mine, got, mats, q):
    height, width = mine.shape
    n = len(q)

    def body(*refs):
        mine_ref, got_ref = refs[:2]
        mat_refs, q_refs = refs[2 : 2 + n], refs[2 + n : 2 + 2 * n]
        out, source = refs[2 + 2 * n :]
        place = position()

        def store(rows, value):
            out[rows, :] = value

        @pl.when(jnp.logical_or(place == span - 1, place == span))
        def _():
            merge_tip(place == span - 1, q_refs, parts_of(mat_refs), height, mine_ref, got_ref, source, store)

    (tip,) = call(
        body,
        [jax.ShapeDtypeStruct((height, width), jnp.bfloat16)],
        [pltpu.VMEM((height, width), jnp.bfloat16)],
        mine, got, *mats, *q,
        flops=2 * product_flops(height, width),
    )
    return tip


def pick(use_new, new, old):
    def body(new_ref, old_ref, out):
        @pl.when(use_new())
        def _():
            out[...] = new_ref[...]

        @pl.when(jnp.logical_not(use_new()))
        def _():
            out[...] = old_ref[...]

    (out,) = call(body, [jax.ShapeDtypeStruct(old.shape, old.dtype)], [], new, old)
    return out


def tip_update(use_new, state, new_tip, tip, spikes, level, merge=()):
    height, width = state.shape
    n = len(spikes)
    kinds = (jnp.float32, jnp.bfloat16) if merge else (jnp.float32,)

    def body(*refs):
        state_ref, new_ref, tip_ref = refs[:3]
        spike_refs, merge_refs = refs[3 : 3 + n], refs[3 + n : 3 + n + len(merge)]
        outs, source = refs[3 + n + len(merge) : -1], refs[-1]

        @pl.when(use_new())
        def _():
            source[...] = new_ref[...]

        @pl.when(jnp.logical_not(use_new()))
        def _():
            source[...] = tip_ref[...]

        starts = row_starts(height, n, 1)
        for rows, value in each_product(at_level(spike_refs, level), starts, source[...]):
            outs[0][rows, :] = state_ref[rows, :] - value
        if not merge:
            return
        source[...] = outs[0][...].astype(jnp.bfloat16)

        def store(rows, value):
            outs[1][rows, :] = value

        send_field(True, merge_refs, height, source, store)

    return call(
        body,
        [jax.ShapeDtypeStruct((height, width), t) for t in kinds],
        [pltpu.VMEM((height, width), jnp.bfloat16)],
        state, new_tip, tip, *spikes, *merge,
        flops=product_flops(height, width),
    )


def last_update(use_new, done, state, new_tip, tip, spikes, level):
    height, width = state.shape
    n, k = len(spikes), len(done)
    own = width // 2
    before = sum(d.shape[1] // 2 for d in done)
    columns = before + own
    split = before - before % 128

    def body(*refs):
        done_refs = refs[:k]
        state_ref, new_ref, tip_ref = refs[k : k + 3]
        spike_refs = refs[k + 3 : k + 3 + n]
        out, source, whole, sems = refs[k + 3 + n :]

        first = 0
        for d in done_refs:
            w = d.shape[1] // 2
            whole[0, :, pl.ds(first, w)] = d[:, :w]
            whole[1, :, pl.ds(first, w)] = d[:, w:]
            first += w
        copies = []
        if split:
            window = pl.ds(0, split)
            copies.append(pltpu.make_async_copy(whole.at[:, :, window], out.at[:, :, window], sems.at[0]))
            copies[0].start()

        @pl.when(use_new())
        def _():
            source[...] = new_ref[...]

        @pl.when(jnp.logical_not(use_new()))
        def _():
            source[...] = tip_ref[...]

        starts = row_starts(height, n, 1)
        for rows, value in each_product(at_level(spike_refs, level), starts, source[...]):
            new = state_ref[rows, :] - value
            whole[0, rows, pl.ds(before, own)] = new[:, :own]
            whole[1, rows, pl.ds(before, own)] = new[:, own:]
        window = pl.ds(split, columns - split)
        copies.append(pltpu.make_async_copy(whole.at[:, :, window], out.at[:, :, window], sems.at[1]))
        copies[-1].start()
        for copy in copies:
            copy.wait()

    return pl.pallas_call(
        body,
        out_shape=jax.ShapeDtypeStruct((2, height, columns), jnp.float32),
        in_specs=[VMEM] * (k + 3 + n),
        out_specs=pl.BlockSpec(memory_space=pl.ANY),
        scratch_shapes=[
            pltpu.VMEM((height, width), jnp.bfloat16),
            pltpu.VMEM((2, height, columns), jnp.float32),
            pltpu.SemaphoreType.DMA((2,)),
        ],
        compiler_params=pltpu.CompilerParams(vmem_limit_bytes=24 * 2**20),
        cost_estimate=pl.CostEstimate(
            flops=product_flops(height, width), bytes_accessed=12 * height * columns, transcendentals=0
        ),
    )(*done, state, new_tip, tip, *spikes)


def swap(block, pairs):
    return lax.ppermute(block, "slab", pairs + [(b, a) for a, b in pairs])


def per_device(widths, rhs, dinv, spikes, merge_inv):
    slabs = lax.axis_size("slab")
    levels = spikes.shape[2]
    chunks = range(len(widths))

    cols = lax.axis_size("col")
    spike_all = ring_gather(spikes[:, 0], "orb")
    spike_own, merge_own = fetch(spikes[:, 0], merge_inv[:, 0])
    spike_all[0] = spike_own
    pairs = [(i, i + 1) for i in range(0, slabs, 2)]
    first = swap(first_matrix(spike_all, merge_own, levels, cols), pairs)
    inverse = ring_gather(dinv[:, 0], "orb")
    merge = [merge_own] + ring_gather(merge_inv[:, 0], "orb")[1:]
    q_own, later = own_matrix(spike_all, merge_own, levels)
    later = swap(later, [(i, i + 1) for i in range(1, slabs - 1, 2)])
    q = ring_gather(q_own, "orb")
    states, sends, gots = [], [], []
    for c in chunks:
        state, hb = start_state(inverse, rhs[:, 0], sum(widths[:c]), widths[c])
        states.append(state)
        sends.append(first_field(merge, hb))
        gots.append(swap(sends[c], pairs))
    first, _ = lax.optimization_barrier((first, sends[-1]))
    sources = [first_source(sends[0], gots[0], q)]
    *across, _ = lax.optimization_barrier((*ring_gather(first, "col"), sources[0]))
    across = [ring_gather(p, "orb") for p in across]
    first = [across[k][j] for j in range(len(q)) for k in range(cols)]
    later = ring_gather(later, "orb")
    for c in chunks:
        if c:
            mine, _ = lax.optimization_barrier((sends[c], across[-1][-1]))
            sources.append(first_source(mine, gots[c], q))
        states[c], sends[c] = first_level(states[c], sources[c], gots[c], first, spike_all, merge)

    for level in range(1, levels):
        span = 1 << level
        heads = range(0, slabs, 2 * span)

        def position(span=span):
            return lax.rem(lax.axis_index("slab"), 2 * span)

        gots = [swap(sends[c], [(g + span - 1, g + span) for g in heads]) for c in chunks]
        tips = [later_tip(position, span, sends[c], gots[c], later, q) for c in chunks]
        reach = 1
        while reach < span:
            route = []
            for g in heads:
                for j in range(reach):
                    if j + reach < span:
                        route.append((g + span + j, g + span + j + reach))
                        route.append((g + span - 1 - j, g + span - 1 - j - reach))
            moved = [lax.ppermute(tips[c], "slab", route) for c in chunks]

            def is_new(span=span, position=position, reach=reach):
                far = jnp.where(position() >= span, position() - span, span - 1 - position())
                return jnp.logical_and(far >= reach, far < 2 * reach)

            if 2 * reach < span:
                tips = [pick(is_new, moved[c], tips[c]) for c in chunks]
            reach *= 2
        if level < levels - 1:
            for c in chunks:
                states[c], sends[c] = tip_update(is_new, states[c], moved[c], tips[c], spike_all, level, merge)
            continue
        for c in chunks[:-1]:
            (states[c],) = tip_update(is_new, states[c], moved[c], tips[c], spike_all, level)
        c = chunks[-1]
        whole = last_update(is_new, states[:c], states[c], moved[c], tips[c], spike_all, level)
    return whole[:, None]


def chunk_widths(columns):
    total = sum(SHARES)
    if columns * min(SHARES) // total < 64:
        return [columns]
    return [columns * s // total for s in SHARES]


def solution(mesh):
    placed = (
        P(None, ("energy", "slab"), None, ("col", "orb")),
        P(None, ("energy", "slab"), "orb", None),
        P(None, ("energy", "slab"), None, "orb", None),
        P(None, ("energy", "slab"), "orb", None),
    )

    def body(rhs, dinv, spikes, merge_inv):
        return per_device(chunk_widths(rhs.shape[3]), rhs, dinv, spikes, merge_inv)

    return jax.shard_map(
        body,
        mesh=mesh,
        in_specs=placed,
        out_specs=P(None, ("energy", "slab"), None, ("col", "orb")),
        check_vma=False,
    )
```

```python
import jax
import jax.numpy as jnp
from jax import lax
from jax.experimental import pallas as pl
from jax.experimental.pallas import tpu as pltpu
from jax.sharding import PartitionSpec as P

VMEM = pl.BlockSpec(memory_space=pltpu.VMEM)
SHARES = (1, 1)


def ring_gather(block, axis):
    count = lax.axis_size(axis)
    blocks = [block]
    for step in range(1, count):
        blocks.append(lax.ppermute(block, axis, [((i + step) % count, i) for i in range(count)]))
    return blocks


def row_starts(height, orb_count, col_parts):
    orb = lax.axis_index("orb")
    per_orb = height // orb_count
    starts = []
    for j in range(orb_count):
        base = lax.rem(orb + j, orb_count) * per_orb
        if col_parts == 1:
            starts.append(base)
            continue
        col = lax.axis_index("col")
        for k in range(col_parts):
            starts.append(base + lax.rem(col + k, col_parts) * (per_orb // col_parts))
    return starts


def rows_of(start, size):
    return pl.ds(pl.multiple_of(start, size), size)


def turned(field):
    half = field.shape[1] // 2
    return jnp.concatenate([-field[:, half:], field[:, :half]], axis=1)


def at_level(spikes, level):
    return [tuple(lambda s=s, p=p: s[p, level] for p in range(2)) for s in spikes]


def parts_of(pieces):
    return [tuple(lambda m=m, p=p: m[p] for p in range(2)) for m in pieces]


def each_product(pieces, starts, field):
    field_i = turned(field)
    for (real, imag), start in zip(pieces, starts):
        value = jnp.dot(real(), field, preferred_element_type=jnp.float32)
        value += jnp.dot(imag(), field_i, preferred_element_type=jnp.float32)
        yield rows_of(start, value.shape[0]), value


def call(body, outs, scratch, *args, flops=0, aliases=None):
    nbytes = sum(a.size * a.dtype.itemsize for a in args) + sum(o.size * o.dtype.itemsize for o in outs)
    return pl.pallas_call(
        body,
        out_shape=outs,
        in_specs=[VMEM] * len(args),
        out_specs=[VMEM] * len(outs),
        scratch_shapes=scratch,
        compiler_params=pltpu.CompilerParams(vmem_limit_bytes=24 * 2**20),
        cost_estimate=pl.CostEstimate(flops=flops, bytes_accessed=nbytes, transcendentals=0),
    )(*args)


def product_flops(height, width):
    return 2 * 2 * height * height * width


def is_even():
    return lax.rem(lax.axis_index("slab"), 2) == 0


def lowest_bit(number, levels):
    found = jnp.int32(0)
    for level in range(1, levels):
        found = jnp.where(lax.rem(number, 1 << level) == 0, level, found)
    return found


def fetch(*arrays):
    n = len(arrays)

    def body(*refs):
        sems = refs[-1]
        copies = [pltpu.make_async_copy(refs[k], refs[n + k], sems.at[k]) for k in range(n)]
        for copy in copies:
            copy.start()
        for copy in copies:
            copy.wait()

    return pl.pallas_call(
        body,
        out_shape=[jax.ShapeDtypeStruct(a.shape, a.dtype) for a in arrays],
        in_specs=[pl.BlockSpec(memory_space=pl.ANY)] * n,
        out_specs=[VMEM] * n,
        scratch_shapes=[pltpu.SemaphoreType.DMA((n,))],
        compiler_params=pltpu.CompilerParams(vmem_limit_bytes=48 * 2**20),
        cost_estimate=pl.CostEstimate(flops=0, bytes_accessed=2 * sum(a.size * 2 for a in arrays), transcendentals=0),
    )(*arrays)


def start_state(pieces, rhs, first, width):
    height = rhs.shape[1]
    n = len(pieces)

    def body(*refs):
        mats, rhs_ref, (out, out_b) = refs[:n], refs[n], refs[n + 1 :]
        window = pl.ds(first, width)
        field = jnp.concatenate([rhs_ref[0, :, window], rhs_ref[1, :, window]], axis=1)
        for rows, value in each_product(parts_of(mats), row_starts(height, n, 1), field):
            out[rows, :] = value
            out_b[rows, :] = value.astype(jnp.bfloat16)

    outs = [jax.ShapeDtypeStruct((height, 2 * width), t) for t in (jnp.float32, jnp.bfloat16)]
    return call(body, outs, [], *pieces, rhs, flops=product_flops(height, 2 * width))


def send_field(odd_sends_product, merge_refs, height, hb_ref, store):
    n = len(merge_refs)
    left = jnp.logical_xor(is_even(), odd_sends_product)

    @pl.when(left)
    def _():
        for rows, value in each_product(parts_of(merge_refs), row_starts(height, n, 1), hb_ref[...]):
            store(rows, value.astype(jnp.bfloat16))

    @pl.when(jnp.logical_not(left))
    def _():
        store(pl.ds(0, height), hb_ref[...])


def first_matrix(spikes, merge_own, levels, cols):
    n = len(spikes)
    size, height = merge_own.shape[1:]
    share = size // cols
    cut = min(128, height)

    def body(*refs):
        spike_refs, merge_ref, out = refs[:n], refs[n], refs[n + 1]
        rows = rows_of(lax.axis_index("col") * share, share)

        @pl.when(is_even())
        def _():
            own_product(spike_refs, merge_ref, rows, 0, cut, out)

        @pl.when(jnp.logical_not(is_even()))
        def _():
            for p in range(2):
                out[p] = spike_refs[0][p, 0, rows, :]

    (out,) = call(
        body,
        [jax.ShapeDtypeStruct((2, share, height), jnp.bfloat16)],
        [],
        *spikes, merge_own,
        flops=product_flops(height, height) // cols,
    )
    return out


def own_product(spike_refs, merge_ref, rows, level, cut, out):
    n = len(spike_refs)
    height = out.shape[2]
    size = height // n
    starts = row_starts(height, n, 1)
    for k in range(height // cut):
        window = pl.ds(k * cut, cut)
        value = 0.0
        for spike, start in zip(spike_refs, starts):
            field = jnp.concatenate([spike[p, level, :, window] for p in range(2)], axis=1)
            piece = tuple(lambda p=p, start=start: merge_ref[p, rows, rows_of(start, size)] for p in range(2))
            for _, part in each_product([piece], [0], field):
                value += part
        out[0, :, window] = value[:, :cut].astype(jnp.bfloat16)
        out[1, :, window] = value[:, cut:].astype(jnp.bfloat16)


def own_matrix(spikes, merge_own, levels):
    n = len(spikes)
    size, height = merge_own.shape[1:]
    cut = min(128, height)

    def body(*refs):
        spike_refs, merge_ref = refs[:n], refs[n]
        q_out, later = refs[n + 1 :]
        device = lax.axis_index("slab")
        own_product(spike_refs, merge_ref, pl.ds(0, size), lowest_bit(device + 1, levels), cut, q_out)
        level_right = lowest_bit(device, levels)

        @pl.when(is_even())
        def _():
            for p in range(2):
                later[p] = spike_refs[0][p, level_right]

        @pl.when(jnp.logical_not(is_even()))
        def _():
            later[...] = q_out[...]

    return call(
        body,
        [jax.ShapeDtypeStruct((2, size, height), jnp.bfloat16)] * 2,
        [],
        *spikes, merge_own,
        flops=product_flops(height, height),
    )


def first_field(merge, hb):
    height, width = hb.shape
    n = len(merge)

    def body(*refs):
        merge_refs, hb_ref, out = refs[:n], refs[n], refs[n + 1]

        def store(rows, value):
            out[rows, :] = value

        send_field(False, merge_refs, height, hb_ref, store)

    (out,) = call(
        body, [jax.ShapeDtypeStruct(hb.shape, jnp.bfloat16)], [], *merge, hb, flops=product_flops(height, width)
    )
    return out


def source_of(left, q_refs, height, mine, got, source):
    @pl.when(left)
    def _():
        starts = row_starts(height, len(q_refs), 1)
        for rows, value in each_product(parts_of(q_refs), starts, got[pl.ds(0, height), :]):
            source[rows, :] = (mine[rows, :].astype(jnp.float32) - value).astype(jnp.bfloat16)

    @pl.when(jnp.logical_not(left))
    def _():
        source[...] = mine[pl.ds(0, height), :]


def tip_from(mats, orb_count, height, source, got, store):
    starts = row_starts(height, orb_count, len(mats) // orb_count)
    for rows, value in each_product(mats, starts, source[...]):
        store(rows, (got[rows, :].astype(jnp.float32) - value).astype(jnp.bfloat16))


def first_source(mine, got, q):
    height, width = mine.shape
    n = len(q)

    def body(*refs):
        mine_ref, got_ref = refs[:2]
        source_of(is_even(), refs[2 : 2 + n], height, mine_ref, got_ref, refs[2 + n])

    (source,) = call(
        body,
        [jax.ShapeDtypeStruct((height, width), jnp.bfloat16)],
        [],
        mine, got, *q,
        flops=product_flops(height, width),
    )
    return source


def merge_tip(left, q_refs, mats, height, mine, got, source, store):
    source_of(left, q_refs, height, mine, got, source)
    tip_from(mats, len(q_refs), height, source, got, store)


def first_level(state, source, got, mats, spikes, merge):
    height, width = state.shape
    n = len(spikes)

    def body(*refs):
        state_ref, source_ref, got_ref = refs[:3]
        mat_refs, rest = refs[3 : 3 + len(mats)], refs[3 + len(mats) :]
        spike_refs, merge_refs = rest[:n], rest[n : 2 * n]
        out, send, rounded, tip = rest[2 * n :]

        def store_tip(rows, value):
            tip[rows, :] = value

        tip_from(parts_of(mat_refs), n, height, source_ref, got_ref, store_tip)
        for rows, value in each_product(at_level(spike_refs, 0), row_starts(height, n, 1), tip[...]):
            new = state_ref[rows, :] - value
            out[rows, :] = new
            rounded[rows, :] = new.astype(jnp.bfloat16)

        def store(rows, value):
            send[rows, :] = value

        send_field(True, merge_refs, height, rounded, store)

    return call(
        body,
        [jax.ShapeDtypeStruct((height, width), t) for t in (jnp.float32, jnp.bfloat16)],
        [pltpu.VMEM((height, width), jnp.bfloat16)] * 2,
        state, source, got, *mats, *spikes, *merge,
        flops=3 * product_flops(height, width),
    )


def later_tip(position, span, mine, got, mats, q):
    height, width = mine.shape
    n = len(q)

    def body(*refs):
        mine_ref, got_ref = refs[:2]
        mat_refs, q_refs = refs[2 : 2 + n], refs[2 + n : 2 + 2 * n]
        out, source = refs[2 + 2 * n :]
        place = position()

        def store(rows, value):
            out[rows, :] = value

        @pl.when(jnp.logical_or(place == span - 1, place == span))
        def _():
            merge_tip(place == span - 1, q_refs, parts_of(mat_refs), height, mine_ref, got_ref, source, store)

    (tip,) = call(
        body,
        [jax.ShapeDtypeStruct((height, width), jnp.bfloat16)],
        [pltpu.VMEM((height, width), jnp.bfloat16)],
        mine, got, *mats, *q,
        flops=2 * product_flops(height, width),
    )
    return tip


def pick(use_new, new, old):
    def body(new_ref, old_ref, out):
        @pl.when(use_new())
        def _():
            out[...] = new_ref[...]

        @pl.when(jnp.logical_not(use_new()))
        def _():
            out[...] = old_ref[...]

    (out,) = call(body, [jax.ShapeDtypeStruct(old.shape, old.dtype)], [], new, old)
    return out


def tip_update(use_new, state, new_tip, tip, spikes, level, merge=()):
    height, width = state.shape
    n = len(spikes)
    kinds = (jnp.float32, jnp.bfloat16) if merge else (jnp.float32,)

    def body(*refs):
        state_ref, new_ref, tip_ref = refs[:3]
        spike_refs, merge_refs = refs[3 : 3 + n], refs[3 + n : 3 + n + len(merge)]
        outs, source = refs[3 + n + len(merge) : -1], refs[-1]

        @pl.when(use_new())
        def _():
            source[...] = new_ref[...]

        @pl.when(jnp.logical_not(use_new()))
        def _():
            source[...] = tip_ref[...]

        starts = row_starts(height, n, 1)
        for rows, value in each_product(at_level(spike_refs, level), starts, source[...]):
            outs[0][rows, :] = state_ref[rows, :] - value
        if not merge:
            return
        source[...] = outs[0][...].astype(jnp.bfloat16)

        def store(rows, value):
            outs[1][rows, :] = value

        send_field(True, merge_refs, height, source, store)

    return call(
        body,
        [jax.ShapeDtypeStruct((height, width), t) for t in kinds],
        [pltpu.VMEM((height, width), jnp.bfloat16)],
        state, new_tip, tip, *spikes, *merge,
        flops=product_flops(height, width),
    )


def last_update(use_new, done, state, new_tip, tip, spikes, level):
    height, width = state.shape
    n, k = len(spikes), len(done)
    own = width // 2
    before = sum(d.shape[1] // 2 for d in done)
    columns = before + own
    split = before - before % 128

    def body(*refs):
        done_refs = refs[:k]
        state_ref, new_ref, tip_ref = refs[k : k + 3]
        spike_refs = refs[k + 3 : k + 3 + n]
        out, source, whole, sems = refs[k + 3 + n :]

        first = 0
        for d in done_refs:
            w = d.shape[1] // 2
            whole[0, :, pl.ds(first, w)] = d[:, :w]
            whole[1, :, pl.ds(first, w)] = d[:, w:]
            first += w
        copies = []
        if split:
            window = pl.ds(0, split)
            copies.append(pltpu.make_async_copy(whole.at[:, :, window], out.at[:, :, window], sems.at[0]))
            copies[0].start()

        @pl.when(use_new())
        def _():
            source[...] = new_ref[...]

        @pl.when(jnp.logical_not(use_new()))
        def _():
            source[...] = tip_ref[...]

        starts = row_starts(height, n, 1)
        for rows, value in each_product(at_level(spike_refs, level), starts, source[...]):
            new = state_ref[rows, :] - value
            whole[0, rows, pl.ds(before, own)] = new[:, :own]
            whole[1, rows, pl.ds(before, own)] = new[:, own:]
        window = pl.ds(split, columns - split)
        copies.append(pltpu.make_async_copy(whole.at[:, :, window], out.at[:, :, window], sems.at[1]))
        copies[-1].start()
        for copy in copies:
            copy.wait()

    return pl.pallas_call(
        body,
        out_shape=jax.ShapeDtypeStruct((2, height, columns), jnp.float32),
        in_specs=[VMEM] * (k + 3 + n),
        out_specs=pl.BlockSpec(memory_space=pl.ANY),
        scratch_shapes=[
            pltpu.VMEM((height, width), jnp.bfloat16),
            pltpu.VMEM((2, height, columns), jnp.float32),
            pltpu.SemaphoreType.DMA((2,)),
        ],
        compiler_params=pltpu.CompilerParams(vmem_limit_bytes=24 * 2**20),
        cost_estimate=pl.CostEstimate(
            flops=product_flops(height, width), bytes_accessed=12 * height * columns, transcendentals=0
        ),
    )(*done, state, new_tip, tip, *spikes)


def last_update_aligned(use_new, done, state, new_tip, tip, spikes, level):
    height, width = state.shape
    n, k = len(spikes), len(done)
    own = width // 2
    before = sum(d.shape[1] // 2 for d in done)
    columns = before + own

    def body(*refs):
        done_refs = refs[:k]
        state_ref, new_ref, tip_ref = refs[k : k + 3]
        spike_refs = refs[k + 3 : k + 3 + n]
        out, source, whole, sems = refs[k + 3 + n :]

        copies = []
        first = 0
        for c, d in enumerate(done_refs):
            w = d.shape[1] // 2
            for p in range(2):
                part = pltpu.make_async_copy(
                    d.at[:, pl.ds(p * w, w)], out.at[p, :, pl.ds(first, w)], sems.at[2 * c + p]
                )
                part.start()
                copies.append(part)
            first += w

        @pl.when(use_new())
        def _():
            source[...] = new_ref[...]

        @pl.when(jnp.logical_not(use_new()))
        def _():
            source[...] = tip_ref[...]

        starts = row_starts(height, n, 1)
        for rows, value in each_product(at_level(spike_refs, level), starts, source[...]):
            new = state_ref[rows, :] - value
            whole[0, rows, :] = new[:, :own]
            whole[1, rows, :] = new[:, own:]
        copies.append(pltpu.make_async_copy(whole, out.at[:, :, pl.ds(before, own)], sems.at[2 * k]))
        copies[-1].start()
        for copy in copies:
            copy.wait()

    return pl.pallas_call(
        body,
        out_shape=jax.ShapeDtypeStruct((2, height, columns), jnp.float32),
        in_specs=[VMEM] * (k + 3 + n),
        out_specs=pl.BlockSpec(memory_space=pl.ANY),
        scratch_shapes=[
            pltpu.VMEM((height, width), jnp.bfloat16),
            pltpu.VMEM((2, height, own), jnp.float32),
            pltpu.SemaphoreType.DMA((2 * k + 1,)),
        ],
        compiler_params=pltpu.CompilerParams(vmem_limit_bytes=24 * 2**20),
        cost_estimate=pl.CostEstimate(
            flops=product_flops(height, width), bytes_accessed=12 * height * columns, transcendentals=0
        ),
    )(*done, state, new_tip, tip, *spikes)


def swap(block, pairs):
    return lax.ppermute(block, "slab", pairs + [(b, a) for a, b in pairs])


def per_device(widths, rhs, dinv, spikes, merge_inv):
    slabs = lax.axis_size("slab")
    levels = spikes.shape[2]
    chunks = range(len(widths))

    cols = lax.axis_size("col")
    spike_all = ring_gather(spikes[:, 0], "orb")
    spike_own, merge_own = fetch(spikes[:, 0], merge_inv[:, 0])
    spike_all[0] = spike_own
    pairs = [(i, i + 1) for i in range(0, slabs, 2)]
    first = swap(first_matrix(spike_all, merge_own, levels, cols), pairs)
    inverse = ring_gather(dinv[:, 0], "orb")
    merge = [merge_own] + ring_gather(merge_inv[:, 0], "orb")[1:]
    q_own, later = own_matrix(spike_all, merge_own, levels)
    later = swap(later, [(i, i + 1) for i in range(1, slabs - 1, 2)])
    q = ring_gather(q_own, "orb")
    states, sends, gots = [], [], []
    for c in chunks:
        state, hb = start_state(inverse, rhs[:, 0], sum(widths[:c]), widths[c])
        states.append(state)
        sends.append(first_field(merge, hb))
        gots.append(swap(sends[c], pairs))
    first, _ = lax.optimization_barrier((first, sends[-1]))
    sources = [first_source(sends[0], gots[0], q)]
    *across, _ = lax.optimization_barrier((*ring_gather(first, "col"), sources[0]))
    across = [ring_gather(p, "orb") for p in across]
    first = [across[k][j] for j in range(len(q)) for k in range(cols)]
    later = ring_gather(later, "orb")
    for c in chunks:
        if c:
            mine, _ = lax.optimization_barrier((sends[c], across[-1][-1]))
            sources.append(first_source(mine, gots[c], q))
        states[c], sends[c] = first_level(states[c], sources[c], gots[c], first, spike_all, merge)

    for level in range(1, levels):
        span = 1 << level
        heads = range(0, slabs, 2 * span)

        def position(span=span):
            return lax.rem(lax.axis_index("slab"), 2 * span)

        gots = [swap(sends[c], [(g + span - 1, g + span) for g in heads]) for c in chunks]
        tips = [later_tip(position, span, sends[c], gots[c], later, q) for c in chunks]
        reach = 1
        while reach < span:
            route = []
            for g in heads:
                for j in range(reach):
                    if j + reach < span:
                        route.append((g + span + j, g + span + j + reach))
                        route.append((g + span - 1 - j, g + span - 1 - j - reach))
            moved = [lax.ppermute(tips[c], "slab", route) for c in chunks]

            def is_new(span=span, position=position, reach=reach):
                far = jnp.where(position() >= span, position() - span, span - 1 - position())
                return jnp.logical_and(far >= reach, far < 2 * reach)

            if 2 * reach < span:
                tips = [pick(is_new, moved[c], tips[c]) for c in chunks]
            reach *= 2
        if level < levels - 1:
            for c in chunks:
                states[c], sends[c] = tip_update(is_new, states[c], moved[c], tips[c], spike_all, level, merge)
            continue
        for c in chunks[:-1]:
            (states[c],) = tip_update(is_new, states[c], moved[c], tips[c], spike_all, level)
        c = chunks[-1]
        aligned = all(w % 128 == 0 for w in widths)
        whole = (last_update_aligned if aligned else last_update)(is_new, states[:c], states[c], moved[c], tips[c], spike_all, level)
    return whole[:, None]


def chunk_widths(columns):
    total = sum(SHARES)
    if columns * min(SHARES) // total < 64:
        return [columns]
    return [columns * s // total for s in SHARES]


def solution(mesh):
    placed = (
        P(None, ("energy", "slab"), None, ("col", "orb")),
        P(None, ("energy", "slab"), "orb", None),
        P(None, ("energy", "slab"), None, "orb", None),
        P(None, ("energy", "slab"), "orb", None),
    )

    def body(rhs, dinv, spikes, merge_inv):
        return per_device(chunk_widths(rhs.shape[3]), rhs, dinv, spikes, merge_inv)

    return jax.shard_map(
        body,
        mesh=mesh,
        in_specs=placed,
        out_specs=P(None, ("energy", "slab"), None, ("col", "orb")),
        check_vma=False,
    )
```

```python
import jax
import jax.numpy as jnp
from jax import lax
from jax.experimental import pallas as pl
from jax.experimental.pallas import tpu as pltpu
from jax.sharding import PartitionSpec as P

VMEM = pl.BlockSpec(memory_space=pltpu.VMEM)
SHARES = (1, 1)


def ring_gather(block, axis):
    count = lax.axis_size(axis)
    blocks = [block]
    for step in range(1, count):
        blocks.append(lax.ppermute(block, axis, [((i + step) % count, i) for i in range(count)]))
    return blocks


def row_starts(height, orb_count, col_parts):
    orb = lax.axis_index("orb")
    per_orb = height // orb_count
    starts = []
    for j in range(orb_count):
        base = lax.rem(orb + j, orb_count) * per_orb
        if col_parts == 1:
            starts.append(base)
            continue
        col = lax.axis_index("col")
        for k in range(col_parts):
            starts.append(base + lax.rem(col + k, col_parts) * (per_orb // col_parts))
    return starts


def rows_of(start, size):
    return pl.ds(pl.multiple_of(start, size), size)


def turned(field):
    half = field.shape[1] // 2
    return jnp.concatenate([-field[:, half:], field[:, :half]], axis=1)


def at_level(spikes, level):
    return [tuple(lambda s=s, p=p: s[p, level] for p in range(2)) for s in spikes]


def parts_of(pieces):
    return [tuple(lambda m=m, p=p: m[p] for p in range(2)) for m in pieces]


def each_product(pieces, starts, field):
    field_i = turned(field)
    for (real, imag), start in zip(pieces, starts):
        value = jnp.dot(real(), field, preferred_element_type=jnp.float32)
        value += jnp.dot(imag(), field_i, preferred_element_type=jnp.float32)
        yield rows_of(start, value.shape[0]), value


def call(body, outs, scratch, *args, flops=0, aliases=None):
    nbytes = sum(a.size * a.dtype.itemsize for a in args) + sum(o.size * o.dtype.itemsize for o in outs)
    return pl.pallas_call(
        body,
        out_shape=outs,
        in_specs=[VMEM] * len(args),
        out_specs=[VMEM] * len(outs),
        scratch_shapes=scratch,
        compiler_params=pltpu.CompilerParams(vmem_limit_bytes=24 * 2**20),
        cost_estimate=pl.CostEstimate(flops=flops, bytes_accessed=nbytes, transcendentals=0),
    )(*args)


def product_flops(height, width):
    return 2 * 2 * height * height * width


def is_even():
    return lax.rem(lax.axis_index("slab"), 2) == 0


def lowest_bit(number, levels):
    found = jnp.int32(0)
    for level in range(1, levels):
        found = jnp.where(lax.rem(number, 1 << level) == 0, level, found)
    return found


def fetch(*arrays):
    n = len(arrays)

    def body(*refs):
        sems = refs[-1]
        copies = [pltpu.make_async_copy(refs[k], refs[n + k], sems.at[k]) for k in range(n)]
        for copy in copies:
            copy.start()
        for copy in copies:
            copy.wait()

    return pl.pallas_call(
        body,
        out_shape=[jax.ShapeDtypeStruct(a.shape, a.dtype) for a in arrays],
        in_specs=[pl.BlockSpec(memory_space=pl.ANY)] * n,
        out_specs=[VMEM] * n,
        scratch_shapes=[pltpu.SemaphoreType.DMA((n,))],
        compiler_params=pltpu.CompilerParams(vmem_limit_bytes=48 * 2**20),
        cost_estimate=pl.CostEstimate(flops=0, bytes_accessed=2 * sum(a.size * 2 for a in arrays), transcendentals=0),
    )(*arrays)


def start_state(pieces, rhs, first, width):
    height = rhs.shape[1]
    n = len(pieces)

    def body(*refs):
        mats, rhs_ref, (out, out_b) = refs[:n], refs[n], refs[n + 1 :]
        window = pl.ds(first, width)
        field = jnp.concatenate([rhs_ref[0, :, window], rhs_ref[1, :, window]], axis=1)
        for rows, value in each_product(parts_of(mats), row_starts(height, n, 1), field):
            out[rows, :] = value
            out_b[rows, :] = value.astype(jnp.bfloat16)

    outs = [jax.ShapeDtypeStruct((height, 2 * width), t) for t in (jnp.float32, jnp.bfloat16)]
    return call(body, outs, [], *pieces, rhs, flops=product_flops(height, 2 * width))


def send_field(odd_sends_product, merge_refs, height, hb_ref, store):
    n = len(merge_refs)
    left = jnp.logical_xor(is_even(), odd_sends_product)

    @pl.when(left)
    def _():
        for rows, value in each_product(parts_of(merge_refs), row_starts(height, n, 1), hb_ref[...]):
            store(rows, value.astype(jnp.bfloat16))

    @pl.when(jnp.logical_not(left))
    def _():
        store(pl.ds(0, height), hb_ref[...])


def first_matrix(spikes, merge_own, levels, cols):
    n = len(spikes)
    size, height = merge_own.shape[1:]
    share = size // cols
    cut = min(128, height)

    def body(*refs):
        spike_refs, merge_ref, out = refs[:n], refs[n], refs[n + 1]
        rows = rows_of(lax.axis_index("col") * share, share)

        @pl.when(is_even())
        def _():
            own_product(spike_refs, merge_ref, rows, 0, cut, out)

        @pl.when(jnp.logical_not(is_even()))
        def _():
            for p in range(2):
                out[p] = spike_refs[0][p, 0, rows, :]

    (out,) = call(
        body,
        [jax.ShapeDtypeStruct((2, share, height), jnp.bfloat16)],
        [],
        *spikes, merge_own,
        flops=product_flops(height, height) // cols,
    )
    return out


def own_product(spike_refs, merge_ref, rows, level, cut, out):
    n = len(spike_refs)
    height = out.shape[2]
    size = height // n
    starts = row_starts(height, n, 1)
    for k in range(height // cut):
        window = pl.ds(k * cut, cut)
        value = 0.0
        for spike, start in zip(spike_refs, starts):
            field = jnp.concatenate([spike[p, level, :, window] for p in range(2)], axis=1)
            piece = tuple(lambda p=p, start=start: merge_ref[p, rows, rows_of(start, size)] for p in range(2))
            for _, part in each_product([piece], [0], field):
                value += part
        out[0, :, window] = value[:, :cut].astype(jnp.bfloat16)
        out[1, :, window] = value[:, cut:].astype(jnp.bfloat16)


def own_matrix(spikes, merge_own, levels):
    n = len(spikes)
    size, height = merge_own.shape[1:]
    cut = min(128, height)

    def body(*refs):
        spike_refs, merge_ref = refs[:n], refs[n]
        q_out, later = refs[n + 1 :]
        device = lax.axis_index("slab")
        own_product(spike_refs, merge_ref, pl.ds(0, size), lowest_bit(device + 1, levels), cut, q_out)
        level_right = lowest_bit(device, levels)

        @pl.when(is_even())
        def _():
            for p in range(2):
                later[p] = spike_refs[0][p, level_right]

        @pl.when(jnp.logical_not(is_even()))
        def _():
            later[...] = q_out[...]

    return call(
        body,
        [jax.ShapeDtypeStruct((2, size, height), jnp.bfloat16)] * 2,
        [],
        *spikes, merge_own,
        flops=product_flops(height, height),
    )


def first_field(merge, hb):
    height, width = hb.shape
    n = len(merge)

    def body(*refs):
        merge_refs, hb_ref, out = refs[:n], refs[n], refs[n + 1]

        def store(rows, value):
            out[rows, :] = value

        send_field(False, merge_refs, height, hb_ref, store)

    (out,) = call(
        body, [jax.ShapeDtypeStruct(hb.shape, jnp.bfloat16)], [], *merge, hb, flops=product_flops(height, width)
    )
    return out


def source_of(left, q_refs, height, mine, got, source):
    @pl.when(left)
    def _():
        starts = row_starts(height, len(q_refs), 1)
        for rows, value in each_product(parts_of(q_refs), starts, got[pl.ds(0, height), :]):
            source[rows, :] = (mine[rows, :].astype(jnp.float32) - value).astype(jnp.bfloat16)

    @pl.when(jnp.logical_not(left))
    def _():
        source[...] = mine[pl.ds(0, height), :]


def tip_from(mats, orb_count, height, source, got, store):
    starts = row_starts(height, orb_count, len(mats) // orb_count)
    for rows, value in each_product(mats, starts, source[...]):
        store(rows, (got[rows, :].astype(jnp.float32) - value).astype(jnp.bfloat16))


def first_source(mine, got, q):
    height, width = mine.shape
    n = len(q)

    def body(*refs):
        mine_ref, got_ref = refs[:2]
        source_of(is_even(), refs[2 : 2 + n], height, mine_ref, got_ref, refs[2 + n])

    (source,) = call(
        body,
        [jax.ShapeDtypeStruct((height, width), jnp.bfloat16)],
        [],
        mine, got, *q,
        flops=product_flops(height, width),
    )
    return source


def merge_tip(left, q_refs, mats, height, mine, got, source, store):
    source_of(left, q_refs, height, mine, got, source)
    tip_from(mats, len(q_refs), height, source, got, store)


def first_level(state, source, got, mats, spikes, merge):
    height, width = state.shape
    n = len(spikes)

    def body(*refs):
        state_ref, source_ref, got_ref = refs[:3]
        mat_refs, rest = refs[3 : 3 + len(mats)], refs[3 + len(mats) :]
        spike_refs, merge_refs = rest[:n], rest[n : 2 * n]
        out, send, rounded, tip = rest[2 * n :]

        def store_tip(rows, value):
            tip[rows, :] = value

        tip_from(parts_of(mat_refs), n, height, source_ref, got_ref, store_tip)
        for rows, value in each_product(at_level(spike_refs, 0), row_starts(height, n, 1), tip[...]):
            new = state_ref[rows, :] - value
            out[rows, :] = new
            rounded[rows, :] = new.astype(jnp.bfloat16)

        def store(rows, value):
            send[rows, :] = value

        send_field(True, merge_refs, height, rounded, store)

    return call(
        body,
        [jax.ShapeDtypeStruct((height, width), t) for t in (jnp.float32, jnp.bfloat16)],
        [pltpu.VMEM((height, width), jnp.bfloat16)] * 2,
        state, source, got, *mats, *spikes, *merge,
        flops=3 * product_flops(height, width),
    )


def later_tip(position, span, mine, got, mats, q):
    height, width = mine.shape
    n = len(q)

    def body(*refs):
        mine_ref, got_ref = refs[:2]
        mat_refs, q_refs = refs[2 : 2 + n], refs[2 + n : 2 + 2 * n]
        out, source = refs[2 + 2 * n :]
        place = position()

        def store(rows, value):
            out[rows, :] = value

        @pl.when(jnp.logical_or(place == span - 1, place == span))
        def _():
            merge_tip(place == span - 1, q_refs, parts_of(mat_refs), height, mine_ref, got_ref, source, store)

    (tip,) = call(
        body,
        [jax.ShapeDtypeStruct((height, width), jnp.bfloat16)],
        [pltpu.VMEM((height, width), jnp.bfloat16)],
        mine, got, *mats, *q,
        flops=2 * product_flops(height, width),
    )
    return tip


def pick(use_new, new, old):
    def body(new_ref, old_ref, out):
        @pl.when(use_new())
        def _():
            out[...] = new_ref[...]

        @pl.when(jnp.logical_not(use_new()))
        def _():
            out[...] = old_ref[...]

    (out,) = call(body, [jax.ShapeDtypeStruct(old.shape, old.dtype)], [], new, old)
    return out


def tip_update(use_new, state, new_tip, tip, spikes, level, merge=()):
    height, width = state.shape
    n = len(spikes)
    kinds = (jnp.float32, jnp.bfloat16) if merge else (jnp.float32,)

    def body(*refs):
        state_ref, new_ref, tip_ref = refs[:3]
        spike_refs, merge_refs = refs[3 : 3 + n], refs[3 + n : 3 + n + len(merge)]
        outs, source = refs[3 + n + len(merge) : -1], refs[-1]

        @pl.when(use_new())
        def _():
            source[...] = new_ref[...]

        @pl.when(jnp.logical_not(use_new()))
        def _():
            source[...] = tip_ref[...]

        starts = row_starts(height, n, 1)
        for rows, value in each_product(at_level(spike_refs, level), starts, source[...]):
            outs[0][rows, :] = state_ref[rows, :] - value
        if not merge:
            return
        source[...] = outs[0][...].astype(jnp.bfloat16)

        def store(rows, value):
            outs[1][rows, :] = value

        send_field(True, merge_refs, height, source, store)

    return call(
        body,
        [jax.ShapeDtypeStruct((height, width), t) for t in kinds],
        [pltpu.VMEM((height, width), jnp.bfloat16)],
        state, new_tip, tip, *spikes, *merge,
        flops=product_flops(height, width),
    )


def last_update(use_new, done, state, new_tip, tip, spikes, level):
    height, width = state.shape
    n, k = len(spikes), len(done)
    own = width // 2
    before = sum(d.shape[1] // 2 for d in done)
    columns = before + own
    split = before - before % 128

    def body(*refs):
        done_refs = refs[:k]
        state_ref, new_ref, tip_ref = refs[k : k + 3]
        spike_refs = refs[k + 3 : k + 3 + n]
        out, source, whole, sems = refs[k + 3 + n :]

        first = 0
        for d in done_refs:
            w = d.shape[1] // 2
            whole[0, :, pl.ds(first, w)] = d[:, :w]
            whole[1, :, pl.ds(first, w)] = d[:, w:]
            first += w
        copies = []
        if split:
            window = pl.ds(0, split)
            copies.append(pltpu.make_async_copy(whole.at[:, :, window], out.at[:, :, window], sems.at[0]))
            copies[0].start()

        @pl.when(use_new())
        def _():
            source[...] = new_ref[...]

        @pl.when(jnp.logical_not(use_new()))
        def _():
            source[...] = tip_ref[...]

        starts = row_starts(height, n, 1)
        for rows, value in each_product(at_level(spike_refs, level), starts, source[...]):
            new = state_ref[rows, :] - value
            whole[0, rows, pl.ds(before, own)] = new[:, :own]
            whole[1, rows, pl.ds(before, own)] = new[:, own:]
        window = pl.ds(split, columns - split)
        copies.append(pltpu.make_async_copy(whole.at[:, :, window], out.at[:, :, window], sems.at[1]))
        copies[-1].start()
        for copy in copies:
            copy.wait()

    return pl.pallas_call(
        body,
        out_shape=jax.ShapeDtypeStruct((2, height, columns), jnp.float32),
        in_specs=[VMEM] * (k + 3 + n),
        out_specs=pl.BlockSpec(memory_space=pl.ANY),
        scratch_shapes=[
            pltpu.VMEM((height, width), jnp.bfloat16),
            pltpu.VMEM((2, height, columns), jnp.float32),
            pltpu.SemaphoreType.DMA((2,)),
        ],
        compiler_params=pltpu.CompilerParams(vmem_limit_bytes=24 * 2**20),
        cost_estimate=pl.CostEstimate(
            flops=product_flops(height, width), bytes_accessed=12 * height * columns, transcendentals=0
        ),
    )(*done, state, new_tip, tip, *spikes)


def last_update_aligned(use_new, done, state, new_tip, tip, spikes, level):
    height, width = state.shape
    n, k = len(spikes), len(done)
    own = width // 2
    before = sum(d.shape[1] // 2 for d in done)
    columns = before + own

    def body(*refs):
        done_refs = refs[:k]
        state_ref, new_ref, tip_ref = refs[k : k + 3]
        spike_refs = refs[k + 3 : k + 3 + n]
        out, whole, sems = refs[k + 3 + n :]

        copies = []
        first = 0
        for c, d in enumerate(done_refs):
            w = d.shape[1] // 2
            for p in range(2):
                part = pltpu.make_async_copy(
                    d.at[:, pl.ds(p * w, w)], out.at[p, :, pl.ds(first, w)], sems.at[2 * c + p]
                )
                part.start()
                copies.append(part)
            first += w

        def update(source):
            starts = row_starts(height, n, 1)
            for rows, value in each_product(at_level(spike_refs, level), starts, source[...]):
                new = state_ref[rows, :] - value
                whole[0, rows, :] = new[:, :own]
                whole[1, rows, :] = new[:, own:]

        @pl.when(use_new())
        def _():
            update(new_ref)

        @pl.when(jnp.logical_not(use_new()))
        def _():
            update(tip_ref)

        copies.append(pltpu.make_async_copy(whole, out.at[:, :, pl.ds(before, own)], sems.at[2 * k]))
        copies[-1].start()
        for copy in copies:
            copy.wait()

    return pl.pallas_call(
        body,
        out_shape=jax.ShapeDtypeStruct((2, height, columns), jnp.float32),
        in_specs=[VMEM] * (k + 3 + n),
        out_specs=pl.BlockSpec(memory_space=pl.ANY),
        scratch_shapes=[
            pltpu.VMEM((2, height, own), jnp.float32),
            pltpu.SemaphoreType.DMA((2 * k + 1,)),
        ],
        compiler_params=pltpu.CompilerParams(vmem_limit_bytes=24 * 2**20),
        cost_estimate=pl.CostEstimate(
            flops=product_flops(height, width), bytes_accessed=12 * height * columns, transcendentals=0
        ),
    )(*done, state, new_tip, tip, *spikes)


def swap(block, pairs):
    return lax.ppermute(block, "slab", pairs + [(b, a) for a, b in pairs])


def per_device(widths, rhs, dinv, spikes, merge_inv):
    slabs = lax.axis_size("slab")
    levels = spikes.shape[2]
    chunks = range(len(widths))

    cols = lax.axis_size("col")
    spike_all = ring_gather(spikes[:, 0], "orb")
    spike_own, merge_own = fetch(spikes[:, 0], merge_inv[:, 0])
    spike_all[0] = spike_own
    pairs = [(i, i + 1) for i in range(0, slabs, 2)]
    first = swap(first_matrix(spike_all, merge_own, levels, cols), pairs)
    inverse = ring_gather(dinv[:, 0], "orb")
    merge = [merge_own] + ring_gather(merge_inv[:, 0], "orb")[1:]
    q_own, later = own_matrix(spike_all, merge_own, levels)
    later = swap(later, [(i, i + 1) for i in range(1, slabs - 1, 2)])
    q = ring_gather(q_own, "orb")
    states, sends, gots = [], [], []
    for c in chunks:
        state, hb = start_state(inverse, rhs[:, 0], sum(widths[:c]), widths[c])
        states.append(state)
        sends.append(first_field(merge, hb))
        gots.append(swap(sends[c], pairs))
    first, _ = lax.optimization_barrier((first, sends[-1]))
    sources = [first_source(sends[0], gots[0], q)]
    *across, _ = lax.optimization_barrier((*ring_gather(first, "col"), sources[0]))
    across = [ring_gather(p, "orb") for p in across]
    first = [across[k][j] for j in range(len(q)) for k in range(cols)]
    later = ring_gather(later, "orb")
    for c in chunks:
        if c:
            mine, _ = lax.optimization_barrier((sends[c], across[-1][-1]))
            sources.append(first_source(mine, gots[c], q))
        states[c], sends[c] = first_level(states[c], sources[c], gots[c], first, spike_all, merge)

    for level in range(1, levels):
        span = 1 << level
        heads = range(0, slabs, 2 * span)

        def position(span=span):
            return lax.rem(lax.axis_index("slab"), 2 * span)

        gots = [swap(sends[c], [(g + span - 1, g + span) for g in heads]) for c in chunks]
        tips = [later_tip(position, span, sends[c], gots[c], later, q) for c in chunks]
        reach = 1
        while reach < span:
            route = []
            for g in heads:
                for j in range(reach):
                    if j + reach < span:
                        route.append((g + span + j, g + span + j + reach))
                        route.append((g + span - 1 - j, g + span - 1 - j - reach))
            moved = [lax.ppermute(tips[c], "slab", route) for c in chunks]

            def is_new(span=span, position=position, reach=reach):
                far = jnp.where(position() >= span, position() - span, span - 1 - position())
                return jnp.logical_and(far >= reach, far < 2 * reach)

            if 2 * reach < span:
                tips = [pick(is_new, moved[c], tips[c]) for c in chunks]
            reach *= 2
        if level < levels - 1:
            for c in chunks:
                states[c], sends[c] = tip_update(is_new, states[c], moved[c], tips[c], spike_all, level, merge)
            continue
        for c in chunks[:-1]:
            (states[c],) = tip_update(is_new, states[c], moved[c], tips[c], spike_all, level)
        c = chunks[-1]
        aligned = all(w % 128 == 0 for w in widths)
        whole = (last_update_aligned if aligned else last_update)(is_new, states[:c], states[c], moved[c], tips[c], spike_all, level)
    return whole[:, None]


def chunk_widths(columns):
    total = sum(SHARES)
    if columns * min(SHARES) // total < 64:
        return [columns]
    return [columns * s // total for s in SHARES]


def solution(mesh):
    placed = (
        P(None, ("energy", "slab"), None, ("col", "orb")),
        P(None, ("energy", "slab"), "orb", None),
        P(None, ("energy", "slab"), None, "orb", None),
        P(None, ("energy", "slab"), "orb", None),
    )

    def body(rhs, dinv, spikes, merge_inv):
        return per_device(chunk_widths(rhs.shape[3]), rhs, dinv, spikes, merge_inv)

    return jax.shard_map(
        body,
        mesh=mesh,
        in_specs=placed,
        out_specs=P(None, ("energy", "slab"), None, ("col", "orb")),
        check_vma=False,
    )
```
